512 devices in a mesh: pipe: 64 (over x, z_hi, y), head: 8 (over z_lo, core).
Axes of the slice: x: 4, y: 8, z: 8 (z_hi: 2, z_lo: 4; z = z_hi * 4 + z_lo), core: 2. Of those that a mesh axis runs over, the one named last changes fastest.
Arguments:
- fresh_qkv: bfloat16 [8192, 9216], P(('pipe', 'head')), may hold values from -6 to 6
- stale_kv: bfloat16 [2, 8192, 3072], P(None, 'pipe', 'head'), may hold values from -20 to 20
- text_kv: bfloat16 [2, 512, 3072], P(None, None, 'head'), may hold values from -12 to 12
- text_len: int32 [1], replicated, may hold values from 64 to 512
- q_gain: float32 [128], replicated, may hold values from 0.5 to 3
- k_gain: float32 [128], replicated, may hold values from 0.5 to 3
- out_weight: bfloat16 [3072, 3072], P('head'), may hold values from -0.15625 to 0.15625
- hidden: bfloat16 [8192, 3072], P(('pipe', 'head')), may hold values from -0.796875 to 0.796875
- gate: float32 [3072], replicated, may hold values from 1 to 8
Outputs:
- updated: bfloat16 [8192, 3072], P(('pipe', 'head'))
The draws below stay inside these ranges and needn't reach their ends.
All inputs are finite; a program needn't handle non-finite values.
Results may differ from the reference program's by a relative error of at most 0.0082.
Values may be sent and summed in bfloat16 or wider, within the bound.
A program may use at most 64 MiB of HBM per device.

```python
import math
import jax
import jax.numpy as jnp
from jax import lax

D = 3072
HEADS = 24
HEAD_DIM = 128
TEXT = 512
PATCH_DEV = 128
TOKENS = 8192
N_PIPE = 64


def walsh_sign(index, level):
    sign = jnp.ones(index.shape, jnp.float32)
    for place in range(3):
        if level >> place & 1:
            sign = sign * (1.0 - 2.0 * (index >> place & 1).astype(jnp.float32))
    return sign


def drawn(key):
    chosen = jax.random.permutation(jax.random.fold_in(key, 11), HEADS)[:2].astype(jnp.int32)
    signs = (jax.random.randint(jax.random.fold_in(key, 12), (2, HEAD_DIM), 0, 2) * 2 - 1).astype(jnp.float32)
    index = jnp.arange(HEAD_DIM, dtype=jnp.int32)
    walsh = jnp.stack([walsh_sign(index, level) for level in (1, 2, 3, 4)], axis=0)
    return (chosen, signs[:, None, :] * walsh[None, :, :])


def draw_fresh_qkv(key, part):
    chosen, directions = drawn(key)
    key = jax.random.fold_in(key, 3)
    noise = jnp.clip(jax.random.normal(jax.random.fold_in(key, 1), (TOKENS, 3 * HEADS, HEAD_DIM), jnp.float32), -6.0, 6.0)
    where = jax.random.randint(jax.random.fold_in(key, 5), (2, 4, 2), 0, TOKENS - PATCH_DEV)
    head_index = jnp.broadcast_to(chosen[:, None, None], (2, 4, 2))
    values = jnp.broadcast_to(directions[:, :, None, :], (2, 4, 2, HEAD_DIM))
    noise = noise.at[where, head_index].set(values)
    return noise.reshape(TOKENS, 3 * D).astype(jnp.bfloat16)


def draw_stale_kv(key, part):
    chosen, directions = drawn(key)
    key = jax.random.fold_in(key, 4)
    noise = jnp.clip(jax.random.normal(jax.random.fold_in(key, 1), (2, TOKENS, HEADS, HEAD_DIM), jnp.float32), -6.0, 6.0)
    largest = 16.0 + 4.0 * (128 // HEAD_DIM)
    levels = jnp.array([0.4, 0.6, 0.8, 1.0], jnp.float32)[:, None] * jnp.array([1.0, 63.0 / 64.0], jnp.float32)[None, :]
    strength = largest * levels
    places = jax.random.permutation(jax.random.fold_in(key, 6), PATCH_DEV)[:8].astype(jnp.int32) + (TOKENS - PATCH_DEV)
    where = jnp.broadcast_to(places.reshape(1, 4, 2), (2, 4, 2))
    head_index = jnp.broadcast_to(chosen[:, None, None], (2, 4, 2))
    values = directions[:, :, None, :] * strength[None, :, :, None]
    stale_keys = (noise[0] * 1.5).at[where, head_index].set(values)
    stacked = jnp.stack([stale_keys, noise[1]], axis=0)
    return stacked.reshape(2, TOKENS, D).astype(jnp.bfloat16)


def spiked(drawn, key, source, target, parts, factor):
    def block_of(axis_at):
        return (jnp.arange(drawn.shape[axis_at]) // (drawn.shape[axis_at] // parts)).reshape((-1,) + (1,) * (drawn.ndim - 1 - axis_at))

    one_side = jax.random.permutation(key, parts)[block_of(target)]
    other_side = (block_of(target) + parts // 2) % parts
    return jnp.where((block_of(source) == one_side) | (block_of(source) == other_side), factor * drawn, drawn)


def level_of(key, dims, pieces, low, high):
    def one(position, parts):
        heights = jax.random.uniform(jax.random.fold_in(jax.random.fold_in(key, 6), position), (parts,), jnp.float32, low / len(pieces), high / len(pieces))
        return jnp.repeat(jnp.exp(heights), dims[position] // parts).reshape((-1,) + (1,) * (len(dims) - position - 1))

    loudness = one(*pieces[0])
    for cut in pieces[1:]:
        loudness = loudness * one(*cut)
    return loudness


def gaussian(rng, shape, spread, limit, pieces=(), kind=jnp.bfloat16):
    values = spread * jax.random.normal(rng, shape, jnp.float32)
    if pieces:
        values = values * level_of(rng, shape, pieces, -0.22, 0.18)
    return jnp.clip(values, -limit, limit).astype(kind)


def heavy_noise(key, extent, spread, bound, pieces, heavy, kind=jnp.bfloat16):
    result = spread * jax.random.normal(key, extent, jnp.float32)
    if pieces:
        result = result * level_of(key, extent, pieces, -0.22, 0.18)
    return jnp.clip(spiked(result, jax.random.fold_in(key, 3), *heavy), -bound, bound).astype(kind)


def setup_inputs(seed: int = 0) -> dict:
    streams_of = jax.random.split(jax.random.key(seed), 10)
    fresh_qkv = draw_fresh_qkv(jax.random.fold_in(streams_of[9], 71), 0)
    stale_kv = draw_stale_kv(jax.random.fold_in(streams_of[9], 71), 0)
    text_kv = gaussian(streams_of[2], (2, TEXT, D), 2.0, 12.0, ((2, 8),))
    text_len = jax.random.randint(streams_of[3], (1,), TEXT // 8, TEXT + 1).astype(jnp.int32)
    q_gain = jnp.clip(jnp.exp(jax.random.uniform(streams_of[4], (HEAD_DIM,), jnp.float32, math.log(0.5), math.log(3.0))), 0.5, 3.0)
    k_gain = jnp.clip(jnp.exp(jax.random.uniform(streams_of[5], (HEAD_DIM,), jnp.float32, math.log(0.5), math.log(3.0))), 0.5, 3.0)
    out_weight = heavy_noise(streams_of[6], (D, D), D ** -0.5, 0.15625, ((0, 8),), (0, 1, 8, 2.0))
    hidden = gaussian(streams_of[7], (TOKENS, D), 0.1, 0.796875, ((0, 512),))
    gate = jnp.clip(jnp.exp(jax.random.uniform(streams_of[8], (D,), jnp.float32, math.log(1.0), math.log(8.0))), 1.0, 8.0)
    return dict(fresh_qkv=fresh_qkv, stale_kv=stale_kv, text_kv=text_kv, text_len=text_len, q_gain=q_gain, k_gain=k_gain, out_weight=out_weight, hidden=hidden, gate=gate)


def rms_scale(values, gain):
    mean_sq = lax.optimization_barrier(jnp.mean(values * values, axis=-1, keepdims=True))
    return values * lax.rsqrt(mean_sq + 1e-06) * gain

def reference(fresh_qkv, stale_kv, text_kv, text_len, q_gain, k_gain, out_weight, hidden, gate):
    split = fresh_qkv.reshape(N_PIPE, PATCH_DEV, 3, HEADS, HEAD_DIM)
    queries = rms_scale(split[:, :, 0].astype(jnp.float32), q_gain).astype(jnp.bfloat16)
    fresh_keys = rms_scale(split[:, :, 1].astype(jnp.float32), k_gain).astype(jnp.bfloat16)
    fresh_values = split[:, :, 2]
    stale_keys = stale_kv[0].reshape(TOKENS, HEADS, HEAD_DIM)
    stale_values = stale_kv[1].reshape(TOKENS, HEADS, HEAD_DIM)
    text_keys = text_kv[0].reshape(TEXT, HEADS, HEAD_DIM)
    text_values = text_kv[1].reshape(TEXT, HEADS, HEAD_DIM)
    valid = jnp.concatenate([jnp.arange(TEXT, dtype=jnp.int32) < text_len[0], jnp.ones((TOKENS,), bool)])
    scale = HEAD_DIM ** (-0.5)

    def one_patch(index):
        start = (index * PATCH_DEV).astype(jnp.int32)
        image_keys = lax.dynamic_update_slice_in_dim(stale_keys, fresh_keys[index], start, 0)
        image_values = lax.dynamic_update_slice_in_dim(stale_values, fresh_values[index], start, 0)
        keys = jnp.concatenate([text_keys, image_keys], axis=0).astype(jnp.float32)
        values = jnp.concatenate([text_values, image_values], axis=0).astype(jnp.float32)
        scores = jnp.einsum('qhd,khd->hqk', queries[index].astype(jnp.float32), keys) * scale
        scores = jnp.where(valid[None, None, :], scores, -1e+30)
        top = lax.optimization_barrier(jnp.max(scores, axis=-1, keepdims=True))
        expo = jnp.exp(scores - top)
        total = lax.optimization_barrier(jnp.sum(expo, axis=-1))
        weights = expo.astype(jnp.bfloat16).astype(jnp.float32)
        summed = jnp.einsum('hqk,khd->qhd', weights, values)
        return (summed / jnp.transpose(total)[:, :, None]).astype(jnp.bfloat16)
    attn = lax.map(one_patch, jnp.arange(N_PIPE, dtype=jnp.int32)).reshape(TOKENS, D)
    projected = jnp.dot(attn, out_weight, preferred_element_type=jnp.float32)
    return (hidden.astype(jnp.float32) + gate * projected).astype(jnp.bfloat16)
```

```python
import math

import jax
import jax.numpy as jnp
from jax import lax
from jax.experimental import pallas as pl
from jax.experimental.pallas import tpu as pltpu
from jax.sharding import PartitionSpec as P

MESH = pl.DeviceIdType.MESH
HD = 128
HEADS = 3
W = HEADS * HD
PATCH = 128
NX, NZ, NY, NL, NC = 4, 2, 8, 4, 2
NH = NL * NC
TOK = PATCH // NH
OWN = NY
D = 3072
CHUNKS = 3
CW = D // CHUNKS
BF, F32 = jnp.bfloat16, jnp.float32


def dot_nt(a, b):
    return lax.dot_general(a, b, (((1,), (1,)), ((), ())), preferred_element_type=F32)


def spread_rows(column):
    return jnp.transpose(jnp.broadcast_to(column, (PATCH, HD)))[0:8]


def split_three(rows):
    hi = rows.astype(BF).astype(F32)
    rest = rows - hi
    mid = rest.astype(BF).astype(F32)
    low = rest - mid
    at = lax.broadcasted_iota(jnp.int32, rows.shape, 0)
    return jnp.where(at == 0, hi, jnp.where(at == 1, mid, jnp.where(at == 2, low, 0.0)))


def merge(parts, logs):
    top = logs[0]
    for row in logs[1:]:
        top = jnp.maximum(top, row)
    shares = [jnp.exp2(row - top) for row in logs]
    total = shares[0]
    for share in shares[1:]:
        total = total + share
    inverse = 1.0 / total
    at = lax.broadcasted_iota(jnp.int32, (8, HD), 0)
    packed = jnp.zeros((8, HD), F32)
    for i, share in enumerate(shares):
        packed = jnp.where(at == i, share * inverse, packed)
    columns = jnp.transpose(jnp.concatenate([packed] * (PATCH // 8), axis=0))
    out = columns[:, 0:1] * parts[0]
    for i in range(1, len(parts)):
        out = out + columns[:, i : i + 1] * parts[i]
    return out, top + jnp.log2(total)


def kernel(
    fresh, stale, text, tlen, qg, kg, w, hidden, gate, o_ref,
    qraw, kvraw, qall, kv, txt, obuf, orecv, zown, zlog, zsend, zrecv, attn, wv, psend, pown, precv, rsend, rrecv,
    loc_sem, q_ssem, q_rsem, f_ssem, f_rsem, kv_ssem, kv_rsem, x_ssem, x_rsem, o_ssem, o_rsem, z_ssem, z_rsem,
    p_ssem, p_rsem, r_ssem, r_rsem,
):
    pipe, me = lax.axis_index("pipe"), lax.axis_index("head")
    x, zh, y = pipe // (NZ * NY), (pipe // NY) % NZ, pipe % NY
    zl, core = me // NC, me % NC

    def at_x(j):
        return ((((x + j) % NX) * NZ + zh) * NY + y, me)

    def at_y(j):
        return ((x * NZ + zh) * NY + (y + j) % NY, me)

    def at_head(r, i):
        return ((x * NZ + (zh + r) % NZ) * NY + y, (me + i) % NH)

    def at_zl(i):
        return (pipe, ((zl + i) % NL) * NC + core)

    pair = (pipe, zl * NC + 1 - core)

    def remote(src, dst, ssem, rsem, dev):
        return pltpu.make_async_remote_copy(
            src_ref=src, dst_ref=dst, send_sem=ssem, recv_sem=rsem, device_id=dev, device_id_type=MESH
        )

    share = x * NZ + zh
    locals_ = [
        pltpu.make_async_copy(w, wv, loc_sem.at[0]),
        pltpu.make_async_copy(
            text.at[:, pl.ds(pl.multiple_of((share // 2) * 128, 128), 128), :], txt, loc_sem.at[1]
        ),
    ]
    own_copies = [
        pltpu.make_async_copy(
            stale.at[:, :, pl.ds(h * HD, HD)], kv.at[h, OWN], loc_sem.at[2 + h]
        )
        for h in range(HEADS)
    ]
    for copy in own_copies + locals_:
        copy.start()

    bar = pltpu.get_barrier_semaphore()
    partners = [at_x(j) for j in range(1, NX)] + [at_y(1), at_y(NY - 1)]
    partners += [at_head(r, i) for r in range(NZ) for i in range(NH) if (r, i) != (0, 0)]
    for dev in partners:
        pl.semaphore_signal(bar, inc=1, device_id=dev, device_id_type=MESH)
    pl.semaphore_wait(bar, len(partners))

    def head_cols(part, i):
        return fresh.at[:, pl.ds(pl.multiple_of(part * D + ((me + i) % NH) * W, W), W)]

    def q_hop(r, i):
        return remote(head_cols(0, i), qraw.at[r, i], q_ssem.at[r, i], q_rsem.at[r, i], at_head(r, i))

    def f_hop(part, i):
        return remote(head_cols(part + 1, i), kvraw.at[part, i], f_ssem.at[part, i], f_rsem.at[part, i], at_head(0, i))

    q_local = pltpu.make_async_copy(head_cols(0, 0), qraw.at[0, 0], q_rsem.at[0, 0])
    f_local = [
        pltpu.make_async_copy(head_cols(part + 1, 0), kvraw.at[part, 0], f_rsem.at[part, 0])
        for part in range(2)
    ]

    q_local.start()
    for r in range(NZ):
        for i in range(NH):
            if (r, i) != (0, 0):
                q_hop(r, i).start()

    def hop(h, slot):
        if slot == 1 or slot == NY - 1:
            src = stale.at[:, :, pl.ds(h * HD, HD)]
        elif slot == 40:
            src = kv.at[h, 3, 0]
        elif slot == 41:
            src = kv.at[h, 5, 1]
        else:
            src = kv.at[h, slot - 1 if slot < 4 else slot + 1]
        if slot >= 40:
            dst = kv.at[h, 4, slot - 40]
        else:
            dst = kv.at[h, slot]
        sem = {40: 0, 41: 4}.get(slot, slot)
        up = slot < 4 or slot == 40
        return remote(src, dst, kv_ssem.at[h, sem], kv_rsem.at[h, sem], at_y(1 if up else NY - 1))

    for h in range(HEADS):
        hop(h, 1).start()
        hop(h, 7).start()

    for part in range(2):
        f_local[part].start()
        for i in range(1, NH):
            f_hop(part, i).start()

    for h in range(HEADS):
        hop(h, 1).wait_recv()
        hop(h, 2).start()
        hop(h, 7).wait_recv()
        hop(h, 6).start()

    scale = math.log2(math.e) / math.sqrt(HD)
    q_local.wait()
    for r in range(NZ):
        for i in range(NH):
            if (r, i) != (0, 0):
                q_hop(r, i).wait_recv()

    def x_hop(h, j):
        return remote(qall.at[h, 0], qall.at[h, NX - j], x_ssem.at[h, j], x_rsem.at[h, NX - j], at_x(j))

    for h in range(HEADS):
        for r in range(NZ):
            q = qraw[r, :, :, pl.ds(h * HD, HD)].reshape(PATCH, HD).astype(F32)
            q = q * lax.rsqrt(jnp.mean(q * q, axis=-1, keepdims=True) + 1e-06)
            qall[h, 0, pl.ds(r * PATCH, PATCH), :] = (q * qg[...]).astype(BF)
        for j in (1, 3, 2):
            x_hop(h, j).start()

    for h in range(HEADS):
        hop(h, 2).wait_recv()
        hop(h, 3).start()
        hop(h, 6).wait_recv()
        hop(h, 5).start()

    for part in range(2):
        f_local[part].wait()
        for i in range(1, NH):
            f_hop(part, i).wait_recv()
    for h in range(HEADS):
        k = kvraw[0, :, :, pl.ds(h * HD, HD)].reshape(PATCH, HD).astype(F32)
        k = k * lax.rsqrt(jnp.mean(k * k, axis=-1, keepdims=True) + 1e-06)
        kv[h, 0, 0] = (k * kg[...]).astype(BF)
        kv[h, 0, 1] = kvraw[1, :, :, pl.ds(h * HD, HD)].reshape(PATCH, HD)

    for h in range(HEADS):
        hop(h, 3).wait_recv()
        hop(h, 40).start()
        hop(h, 5).wait_recv()
        hop(h, 41).start()

    for copy in own_copies:
        copy.wait()
    locals_[1].wait()
    spot = lax.broadcasted_iota(jnp.int32, (1, 128), 1)
    live = (spot // 64 == share % 2) & (spot + (share // 2) * 128 < tlen[0])
    bias = jnp.where(live, 0.0, -1e30)

    def o_hop(h, j):
        return remote(obuf.at[h, j], orecv.at[h, NX - j], o_ssem.at[h, j], o_rsem.at[h, NX - j], at_x(j))

    def z_hop(h):
        return remote(zsend.at[h], zrecv.at[h], z_ssem.at[h], z_rsem.at[h], at_head(1, 0))

    def attend(h, t):
        j = (t + 1) % NX
        stats = []
        for r in range(NZ):
            slots = pl.ds(1 - t // (NX - 1) if r == 0 else 1, NY)
            q = qall[h, j, pl.ds(r * PATCH, PATCH), :]
            scores = dot_nt(q, kv[h, slots, 0].reshape(NY * PATCH, HD))
            tscores = dot_nt(q, txt[0, :, pl.ds(h * HD, HD)]) + bias
            top = jnp.maximum(jnp.max(scores, axis=-1, keepdims=True), jnp.max(tscores, axis=-1, keepdims=True))
            e, te = jnp.exp2((scores - top) * scale), jnp.exp2((tscores - top) * scale)
            total = jnp.sum(e, axis=-1, keepdims=True) + jnp.sum(te, axis=-1, keepdims=True)
            out = jnp.dot(e.astype(BF), kv[h, slots, 1].reshape(NY * PATCH, HD), preferred_element_type=F32)
            out = out + jnp.dot(te.astype(BF), txt[1, :, pl.ds(h * HD, HD)], preferred_element_type=F32)
            obuf[h, j, pl.ds(r * PATCH, PATCH), :] = (out * (1.0 / total)).astype(BF)
            stats.append(split_three(spread_rows(top * scale + jnp.log2(total))))
        obuf[h, j, pl.ds(NZ * PATCH, 16), :] = jnp.concatenate(stats, axis=0).astype(BF)

    def logs_of(packed, r):
        rows = packed.astype(F32)
        return rows[8 * r : 8 * r + 1] + rows[8 * r + 1 : 8 * r + 2] + rows[8 * r + 2 : 8 * r + 3]

    def combine_x(h):
        for j in range(1, NX):
            o_hop(h, j).wait_recv()
        sources = [obuf.at[h, 0]] + [orecv.at[h, j] for j in range(1, NX)]
        for r in (1, 0):
            parts = [s[pl.ds(r * PATCH, PATCH), :].astype(F32) for s in sources]
            logs = [logs_of(s[pl.ds(NZ * PATCH, 16), :], r) for s in sources]
            out, log = merge(parts, logs)
            if r == 1:
                zsend[h, pl.ds(0, PATCH), :] = out.astype(BF)
                packed = split_three(jnp.broadcast_to(log, (8, HD)))
                zsend[h, pl.ds(PATCH, 16), :] = jnp.concatenate([packed, packed], axis=0).astype(BF)
                z_hop(h).start()
            else:
                zown[h] = out
                zlog[h] = jnp.broadcast_to(log, (8, HD))

    for h in range(HEADS):
        for j in range(1, NX):
            x_hop(h, j).wait_recv()
        hop(h, 40).wait_recv()
        hop(h, 41).wait_recv()

        for t in range(NX):
            attend(h, t)
            if t < NX - 1:
                o_hop(h, t + 1).start()
        if h > 0:
            combine_x(h - 1)
    combine_x(HEADS - 1)

    for h in range(HEADS):
        z_hop(h).wait_recv()
        out, _ = merge(
            [zown[h], zrecv[h, pl.ds(0, PATCH), :].astype(F32)],
            [zlog[h, 0:1], logs_of(zrecv[h, pl.ds(PATCH, 16), :], 0)],
        )
        attn[:, :, pl.ds(h * HD, HD)] = out.astype(BF).reshape(NH, TOK, HD)

    locals_[0].wait()
    rows = jnp.concatenate(
        [attn[(me + NH - ((zl + i) % NL) * NC - c) % NH] for c in (1 - core, core) for i in range(NL)], axis=0
    )

    def p_hop(c):
        return remote(psend.at[c], precv.at[c], p_ssem.at[c], p_rsem.at[c], pair)

    def r_hop(c, i):
        return remote(rsend.at[c, i], rrecv.at[c, NL - i], r_ssem.at[c, i], r_rsem.at[c, NL - i], at_zl(i))

    half = NL * TOK
    for c in range(CHUNKS):
        cols = pl.ds(c * CW, CW)
        part = jnp.dot(rows, wv[:, cols], preferred_element_type=F32)
        psend[c] = part[:half].astype(BF)
        p_hop(c).start()
        pown[c] = part[half:]
    for c in range(CHUNKS):
        p_hop(c).wait_recv()
        both = pown[c] + precv[c].astype(F32)
        for i in (2, 1, 3):
            rsend[c, i] = both[i * TOK : (i + 1) * TOK].astype(BF)
            r_hop(c, i).start()
        pown[c, pl.ds(0, TOK), :] = both[:TOK]
    for c in range(CHUNKS):
        cols = pl.ds(c * CW, CW)
        total = pown[c, pl.ds(0, TOK), :]
        for i in range(1, NL):
            r_hop(c, NL - i).wait_recv()
            total = total + rrecv[c, i].astype(F32)
        o_ref[:, cols] = (hidden[:, cols].astype(F32) + gate[:, cols] * total).astype(BF)

    for r in range(2):
        for i in range(NH):
            if (r, i) != (0, 0):
                q_hop(r, i).wait_send()
            if i > 0:
                f_hop(r, i).wait_send()
    for h in range(HEADS):
        for slot in (1, 2, 3, 40, 41, 5, 6, 7):
            hop(h, slot).wait_send()
        for j in range(1, NX):
            x_hop(h, j).wait_send()
            o_hop(h, j).wait_send()
        z_hop(h).wait_send()
    for c in range(CHUNKS):
        p_hop(c).wait_send()
        for i in range(1, NL):
            r_hop(c, i).wait_send()


def on_device(fresh, stale, text, tlen, qg, kg, w, hidden, gate):
    dma = pltpu.SemaphoreType.DMA
    hbm, vmem = pl.BlockSpec(memory_space=pl.ANY), pl.BlockSpec(memory_space=pltpu.VMEM)
    return pl.pallas_call(
        kernel,
        out_shape=jax.ShapeDtypeStruct((TOK, D), BF),
        in_specs=[hbm, hbm, hbm, pl.BlockSpec(memory_space=pltpu.SMEM), vmem, vmem, hbm, vmem, vmem],
        out_specs=vmem,
        scratch_shapes=[
            pltpu.VMEM((NZ, NH, TOK, W), BF),
            pltpu.VMEM((2, NH, TOK, W), BF),
            pltpu.VMEM((HEADS, NX, NZ * PATCH, HD), BF),
            pltpu.VMEM((HEADS, NY + 1, 2, PATCH, HD), BF),
            pltpu.VMEM((2, 128, W), BF),
            pltpu.VMEM((HEADS, NX, NZ * PATCH + 16, HD), BF),
            pltpu.VMEM((HEADS, NX, NZ * PATCH + 16, HD), BF),
            pltpu.VMEM((HEADS, PATCH, HD), F32),
            pltpu.VMEM((HEADS, 8, HD), F32),
            pltpu.VMEM((HEADS, PATCH + 16, HD), BF),
            pltpu.VMEM((HEADS, PATCH + 16, HD), BF),
            pltpu.VMEM((NH, TOK, W), BF),
            pltpu.VMEM((W, D), BF),
            pltpu.VMEM((CHUNKS, NL * TOK, CW), BF),
            pltpu.VMEM((CHUNKS, NL * TOK, CW), F32),
            pltpu.VMEM((CHUNKS, NL * TOK, CW), BF),
            pltpu.VMEM((CHUNKS, NL, TOK, CW), BF),
            pltpu.VMEM((CHUNKS, NL, TOK, CW), BF),
            dma((2 + HEADS,)), dma((NZ, NH)), dma((NZ, NH)), dma((2, NH)), dma((2, NH)), dma((HEADS, NY)), dma((HEADS, NY)),
            dma((HEADS, NX)), dma((HEADS, NX)), dma((HEADS, NX)), dma((HEADS, NX)), dma((HEADS,)), dma((HEADS,)),
            dma((CHUNKS,)), dma((CHUNKS,)), dma((CHUNKS, NL)), dma((CHUNKS, NL)),
        ],
        name="joint_attention",
        cost_estimate=pl.CostEstimate(flops=2 * 10**9, bytes_accessed=4 * 10**6, transcendentals=4 * 10**6),
        compiler_params=pltpu.CompilerParams(
            collective_id=0, has_side_effects=True, vmem_limit_bytes=60 * 2**20
        ),
    )(fresh, stale, text, tlen, qg.reshape(1, HD), kg.reshape(1, HD), w, hidden, gate.reshape(1, D))


def solution(mesh):
    return jax.shard_map(
        on_device,
        mesh=mesh,
        in_specs=(
            P(("pipe", "head"), None),
            P(None, "pipe", "head"),
            P(None, None, "head"),
            P(),
            P(),
            P(),
            P("head", None),
            P(("pipe", "head"), None),
            P(),
        ),
        out_specs=P(("pipe", "head"), None),
        check_vma=False,
    )
```

```python
import math

import jax
import jax.numpy as jnp
from jax import lax
from jax.experimental import pallas as pl
from jax.experimental.pallas import tpu as pltpu
from jax.sharding import PartitionSpec as P

MESH = pl.DeviceIdType.MESH
HD = 128
HEADS = 3
W = HEADS * HD
PATCH = 128
NX, NZ, NY, NL, NC = 4, 2, 8, 4, 2
NH = NL * NC
HALF = PATCH // 2
TOK = PATCH // NH
OWN = NY
D = 3072
CHUNKS = 3
CW = D // CHUNKS
BF, F32 = jnp.bfloat16, jnp.float32


def dot_nt(a, b):
    return lax.dot_general(a, b, (((1,), (1,)), ((), ())), preferred_element_type=F32)


def spread_rows(column):
    return jnp.transpose(jnp.broadcast_to(column, (PATCH, HD)))[0:8]


def split_three(rows):
    hi = rows.astype(BF).astype(F32)
    rest = rows - hi
    mid = rest.astype(BF).astype(F32)
    low = rest - mid
    at = lax.broadcasted_iota(jnp.int32, rows.shape, 0)
    return jnp.where(at == 0, hi, jnp.where(at == 1, mid, jnp.where(at == 2, low, 0.0)))


def merge(parts, logs):
    top = logs[0]
    for row in logs[1:]:
        top = jnp.maximum(top, row)
    shares = [jnp.exp2(row - top) for row in logs]
    total = shares[0]
    for share in shares[1:]:
        total = total + share
    inverse = 1.0 / total
    at = lax.broadcasted_iota(jnp.int32, (8, HD), 0)
    packed = jnp.zeros((8, HD), F32)
    for i, share in enumerate(shares):
        packed = jnp.where(at == i, share * inverse, packed)
    columns = jnp.transpose(jnp.concatenate([packed] * (PATCH // 8), axis=0))[: parts[0].shape[0]]
    out = columns[:, 0:1] * parts[0]
    for i in range(1, len(parts)):
        out = out + columns[:, i : i + 1] * parts[i]
    return out, top + jnp.log2(total)


def kernel(
    fresh, stale, text, tlen, qg_in, kg_in, w, hidden_in, gate_in, o_ref,
    qraw, kvraw, qall, kv, txt, obuf, orecv, zown, zlog, zsend, zrecv, attn, wv, psend, pown, precv, pfin, rsend, rrecv,
    qg, kg, hidden, gate,
    loc_sem, q_ssem, q_rsem, f_ssem, f_rsem, kv_ssem, kv_rsem, x_ssem, x_rsem, o_ssem, o_rsem, z_ssem, z_rsem,
    p_ssem, p_rsem, r_ssem, r_rsem,
):
    pipe, me = lax.axis_index("pipe"), lax.axis_index("head")
    x, zh, y = pipe // (NZ * NY), (pipe // NY) % NZ, pipe % NY
    zl, core = me // NC, me % NC

    def at_x(j):
        return ((((x + j) % NX) * NZ + zh) * NY + y, me)

    def at_y(j):
        return ((x * NZ + zh) * NY + (y + j) % NY, me)

    def at_head(r, i):
        return ((x * NZ + (zh + r) % NZ) * NY + y, (me + i) % NH)

    pair = (pipe, zl * NC + 1 - core)

    def remote(src, dst, ssem, rsem, dev):
        return pltpu.make_async_remote_copy(
            src_ref=src, dst_ref=dst, send_sem=ssem, recv_sem=rsem, device_id=dev, device_id_type=MESH
        )

    bar = pltpu.get_barrier_semaphore()
    partners = [at_x(j) for j in range(1, NX)] + [at_y(1), at_y(NY - 1)]
    partners += [at_head(r, i) for r in range(NZ) for i in range(NH) if (r, i) != (0, 0)]
    for dev in partners:
        pl.semaphore_signal(bar, inc=1, device_id=dev, device_id_type=MESH)

    share = x * NZ + zh
    get_w = pltpu.make_async_copy(w, wv, loc_sem.at[0])
    get_text = pltpu.make_async_copy(
        text.at[:, pl.ds(pl.multiple_of((share // 2) * 128, 128), 128), :], txt, loc_sem.at[1]
    )
    get_small = [
        pltpu.make_async_copy(src, dst, loc_sem.at[2 + n])
        for n, (src, dst) in enumerate(((qg_in, qg), (kg_in, kg), (hidden_in, hidden), (gate_in, gate)))
    ]
    get_own = [
        pltpu.make_async_copy(stale.at[:, :, pl.ds(h * HD, HD)], kv.at[h, OWN], loc_sem.at[6 + h])
        for h in range(HEADS)
    ]

    def head_cols(part, i):
        return fresh.at[:, pl.ds(pl.multiple_of(part * D + ((me + i) % NH) * W, W), W)]

    my_half, my_spot = ((zl + 1) // 2) % 2, (zl // 2) * NC + core

    def q_hop(r, i):
        return remote(
            head_cols(0, i), qraw.at[my_half, r, my_spot], q_ssem.at[r, i], q_rsem.at[r, i], at_head(r, i)
        )

    def f_hop(part, i):
        return remote(head_cols(part + 1, i), kvraw.at[part, i], f_ssem.at[part, i], f_rsem.at[part, i], at_head(0, i))

    q_local = pltpu.make_async_copy(head_cols(0, 0), qraw.at[my_half, 0, my_spot], q_rsem.at[0, 0])
    f_local = [
        pltpu.make_async_copy(head_cols(part + 1, 0), kvraw.at[part, 0], f_rsem.at[part, 0]) for part in range(2)
    ]
    q_local.start()
    for copy in get_small[:2]:
        copy.start()
    pl.semaphore_wait(bar, len(partners))

    for r in (1, 0):
        for i in range(NH):
            if (r, i) != (0, 0):
                q_hop(r, i).start()

    def hop(h, slot):
        if slot == 1 or slot == NY - 1:
            src = stale.at[:, :, pl.ds(h * HD, HD)]
        elif slot == 40:
            src = kv.at[h, 3, 0]
        elif slot == 41:
            src = kv.at[h, 5, 1]
        else:
            src = kv.at[h, slot - 1 if slot < 4 else slot + 1]
        if slot >= 40:
            dst = kv.at[h, 4, slot - 40]
        else:
            dst = kv.at[h, slot]
        sem = {40: 0, 41: 4}.get(slot, slot)
        up = slot < 4 or slot == 40
        return remote(src, dst, kv_ssem.at[h, sem], kv_rsem.at[h, sem], at_y(1 if up else NY - 1))

    for h in range(HEADS):
        hop(h, 1).start()
        hop(h, 7).start()

    for copy in [*get_own, get_text, get_w, *get_small[2:]]:
        copy.start()

    for part in range(2):
        f_local[part].start()
        for i in range(1, NH):
            f_hop(part, i).start()

    for h in range(HEADS):
        hop(h, 1).wait_recv()
        hop(h, 2).start()
        hop(h, 7).wait_recv()
        hop(h, 6).start()

    scale = math.log2(math.e) / math.sqrt(HD)

    def normed(rows, gain):
        return (rows * lax.rsqrt(jnp.mean(rows * rows, axis=-1, keepdims=True) + 1e-06) * gain[...]).astype(BF)

    def x_hop(half, j):
        return remote(
            qall.at[half, 0], qall.at[half, NX - j], x_ssem.at[half, j], x_rsem.at[half, NX - j], at_x(j)
        )

    for copy in get_small[:2]:
        copy.wait()
    q_local.wait()
    for r in range(NZ):
        for i in range(NH):
            if (r, i) != (0, 0):
                q_hop(r, i).wait_recv()
    for half in range(2):
        for h in range(HEADS):
            rows = qraw[half, :, :, :, pl.ds(h * HD, HD)].reshape(PATCH, HD).astype(F32)
            qall[half, 0, h] = normed(rows, qg)
        for j in (2, 1, 3):
            x_hop(half, j).start()

    for h in range(HEADS):
        hop(h, 2).wait_recv()
        hop(h, 3).start()
        hop(h, 6).wait_recv()
        hop(h, 5).start()

    for part in range(2):
        f_local[part].wait()
        for i in range(1, NH):
            f_hop(part, i).wait_recv()
    for h in range(HEADS):
        cols = pl.ds(h * HD, HD)
        kv[h, 0, 0] = normed(kvraw[0, :, :, cols].reshape(PATCH, HD).astype(F32), kg)
        kv[h, 0, 1] = kvraw[1, :, :, cols].reshape(PATCH, HD)

    for h in range(HEADS):
        hop(h, 3).wait_recv()
        hop(h, 40).start()
        hop(h, 5).wait_recv()
        hop(h, 41).start()

    for copy in get_own:
        copy.wait()
    get_text.wait()
    spot = lax.broadcasted_iota(jnp.int32, (1, 128), 1)
    live = (spot // 64 == share % 2) & (spot + (share // 2) * 128 < tlen[0])
    bias = jnp.where(live, 0.0, -1e30)

    def o_hop(half, j):
        return remote(
            obuf.at[half, j], orecv.at[half, NX - j], o_ssem.at[half, j], o_rsem.at[half, NX - j], at_x(j)
        )

    def z_hop(half):
        return remote(zsend.at[half], zrecv.at[half], z_ssem.at[half], z_rsem.at[half], at_head(1, 0))

    def soft(q, h, first):
        slots = pl.ds(first, NY)
        scores = dot_nt(q, kv[h, slots, 0].reshape(NY * PATCH, HD))
        tscores = dot_nt(q, txt[0, :, pl.ds(h * HD, HD)]) + bias
        top = jnp.maximum(jnp.max(scores, axis=-1, keepdims=True), jnp.max(tscores, axis=-1, keepdims=True))
        e, te = jnp.exp2((scores - top) * scale), jnp.exp2((tscores - top) * scale)
        total = jnp.sum(e, axis=-1, keepdims=True) + jnp.sum(te, axis=-1, keepdims=True)
        out = jnp.dot(e.astype(BF), kv[h, slots, 1].reshape(NY * PATCH, HD), preferred_element_type=F32)
        out = out + jnp.dot(te.astype(BF), txt[1, :, pl.ds(h * HD, HD)], preferred_element_type=F32)
        return out * (1.0 / total), top * scale + jnp.log2(total)

    def attend(half, j):
        for h in range(HEADS):
            if j == 0:
                two = [soft(qall[half, 0, h, pl.ds(r * HALF, HALF), :], h, r) for r in range(NZ)]
                out, log = (jnp.concatenate([a, b], axis=0) for a, b in zip(*two))
            else:
                out, log = soft(qall[half, j, h], h, 1)
            obuf[half, j, h, pl.ds(0, PATCH), :] = out.astype(BF)
            obuf[half, j, h, pl.ds(PATCH, 16), :] = packed(spread_rows(log))
        if j > 0:
            o_hop(half, j).start()

    def packed(rows):
        return jnp.concatenate([split_three(rows), jnp.zeros((8, HD), F32)], axis=0).astype(BF)

    def logs_of(rows):
        rows = rows.astype(F32)
        return rows[0:1] + rows[1:2] + rows[2:3]

    def merge_x(half):
        for j in range(1, NX):
            o_hop(half, j).wait_recv()
        for h in range(HEADS):
            sources = [obuf.at[half, 0, h]] + [orecv.at[half, j, h] for j in range(1, NX)]
            parts = [s[pl.ds(0, PATCH), :].astype(F32) for s in sources]
            out, log = merge(parts, [logs_of(s[pl.ds(PATCH, 16), :]) for s in sources])
            log = jnp.broadcast_to(log, (8, HD))
            zsend[half, h, pl.ds(0, HALF), :] = out[HALF:].astype(BF)
            zsend[half, h, pl.ds(HALF, 16), :] = packed(pltpu.roll(log, HALF, 1))
            zown[half, h] = out[:HALF]
            zlog[half, h] = log
        z_hop(half).start()

    def merge_z(half):
        z_hop(half).wait_recv()
        for h in range(HEADS):
            out, _ = merge(
                [zown[half, h], zrecv[half, h, pl.ds(0, HALF), :].astype(F32)],
                [zlog[half, h, 0:1], logs_of(zrecv[half, h, pl.ds(HALF, 16), :])],
            )
            attn[half, :, :, pl.ds(h * HD, HD)] = out.astype(BF).reshape(NH // 2, TOK, HD)

    def p_hop(half, c):
        return remote(psend.at[half, c], precv.at[half, c], p_ssem.at[half, c], p_rsem.at[half, c], pair)

    def project(half):
        rows = jnp.concatenate([attn[half, n * NC + c] for c in (1 - core, core) for n in range(2)], axis=0)
        for c in range(CHUNKS):
            part = jnp.dot(rows, wv[:, pl.ds(c * CW, CW)], preferred_element_type=F32)
            psend[half, c] = part[: 2 * TOK].astype(BF)
            p_hop(half, c).start()
            pown[half, c] = part[2 * TOK :]

    def r_hop(half, c, n):
        owner = ((0, 3), (1, 2))[half][n]
        away = (owner + NL - zl) % NL
        return remote(
            rsend.at[half, c, n], rrecv.at[c, away], r_ssem.at[half, c, n], r_rsem.at[c, away], (pipe, owner * NC + core)
        )

    def arrived(c, away):
        return remote(rsend.at[0, c, 0], rrecv.at[c, away], r_ssem.at[0, c, 0], r_rsem.at[c, away], pair)

    def reduce(half):
        for c in range(CHUNKS):
            p_hop(half, c).wait_recv()
            both = pown[half, c] + precv[half, c].astype(F32)
            for n in range(2):
                owner = ((0, 3), (1, 2))[half][n]
                mine = both[n * TOK : (n + 1) * TOK]
                rsend[half, c, n] = mine.astype(BF)

                @pl.when(zl != owner)
                def _():
                    r_hop(half, c, n).start()

                @pl.when(zl == owner)
                def _():
                    pfin[c] = mine

    for half in range(2):
        for j in range(1, NX):
            x_hop(half, j).wait_recv()
        if half == 0:
            for h in range(HEADS):
                hop(h, 40).wait_recv()
                hop(h, 41).wait_recv()
        for j in (2, 1, 3):
            attend(half, j)
        if half == 1:
            merge_x(0)
        attend(half, 0)
    merge_x(1)
    merge_z(0)
    get_w.wait()
    project(0)
    reduce(0)
    merge_z(1)
    project(1)
    reduce(1)

    for copy in get_small[2:]:
        copy.wait()
    for c in range(CHUNKS):
        cols = pl.ds(c * CW, CW)
        for i in range(1, NL):
            arrived(c, i).wait_recv()
        total = pfin[c]
        for i in range(1, NL):
            total = total + rrecv[c, i].astype(F32)
        o_ref[:, cols] = (hidden[:, cols].astype(F32) + gate[:, cols] * total).astype(BF)

    for r in range(2):
        for i in range(NH):
            if (r, i) != (0, 0):
                q_hop(r, i).wait_send()
            if i > 0:
                f_hop(r, i).wait_send()
    for h in range(HEADS):
        for slot in (1, 2, 3, 40, 41, 5, 6, 7):
            hop(h, slot).wait_send()
    for half in range(2):
        for j in range(1, NX):
            x_hop(half, j).wait_send()
            o_hop(half, j).wait_send()
        z_hop(half).wait_send()
        for c in range(CHUNKS):
            p_hop(half, c).wait_send()
            for n in range(2):

                @pl.when(zl != ((0, 3), (1, 2))[half][n])
                def _():
                    r_hop(half, c, n).wait_send()


def on_device(fresh, stale, text, tlen, qg, kg, w, hidden, gate):
    dma = pltpu.SemaphoreType.DMA
    hbm, vmem = pl.BlockSpec(memory_space=pl.ANY), pl.BlockSpec(memory_space=pltpu.VMEM)
    return pl.pallas_call(
        kernel,
        out_shape=jax.ShapeDtypeStruct((TOK, D), BF),
        in_specs=[hbm, hbm, hbm, pl.BlockSpec(memory_space=pltpu.SMEM), hbm, hbm, hbm, hbm, hbm],
        out_specs=vmem,
        scratch_shapes=[
            pltpu.VMEM((2, NZ, NH // 2, TOK, W), BF),
            pltpu.VMEM((2, NH, TOK, W), BF),
            pltpu.VMEM((2, NX, HEADS, PATCH, HD), BF),
            pltpu.VMEM((HEADS, NY + 1, 2, PATCH, HD), BF),
            pltpu.VMEM((2, 128, W), BF),
            pltpu.VMEM((2, NX, HEADS, PATCH + 16, HD), BF),
            pltpu.VMEM((2, NX, HEADS, PATCH + 16, HD), BF),
            pltpu.VMEM((2, HEADS, HALF, HD), F32),
            pltpu.VMEM((2, HEADS, 8, HD), F32),
            pltpu.VMEM((2, HEADS, HALF + 16, HD), BF),
            pltpu.VMEM((2, HEADS, HALF + 16, HD), BF),
            pltpu.VMEM((2, NH // 2, TOK, W), BF),
            pltpu.VMEM((W, D), BF),
            pltpu.VMEM((2, CHUNKS, 2 * TOK, CW), BF),
            pltpu.VMEM((2, CHUNKS, 2 * TOK, CW), F32),
            pltpu.VMEM((2, CHUNKS, 2 * TOK, CW), BF),
            pltpu.VMEM((CHUNKS, TOK, CW), F32),
            pltpu.VMEM((2, CHUNKS, 2, TOK, CW), BF),
            pltpu.VMEM((CHUNKS, NL, TOK, CW), BF),
            pltpu.VMEM((1, HD), F32),
            pltpu.VMEM((1, HD), F32),
            pltpu.VMEM((TOK, D), BF),
            pltpu.VMEM((1, D), F32),
            dma((6 + HEADS,)), dma((NZ, NH)), dma((NZ, NH)), dma((2, NH)), dma((2, NH)), dma((HEADS, NY)),
            dma((HEADS, NY)), dma((2, NX)), dma((2, NX)), dma((2, NX)), dma((2, NX)), dma((2,)), dma((2,)),
            dma((2, CHUNKS)), dma((2, CHUNKS)), dma((2, CHUNKS, 2)), dma((CHUNKS, NL)),
        ],
        name="joint_attention",
        cost_estimate=pl.CostEstimate(flops=2 * 10**9, bytes_accessed=4 * 10**6, transcendentals=4 * 10**6),
        compiler_params=pltpu.CompilerParams(
            collective_id=0, has_side_effects=True, vmem_limit_bytes=60 * 2**20
        ),
    )(fresh, stale, text, tlen, qg.reshape(1, HD), kg.reshape(1, HD), w, hidden, gate.reshape(1, D))


def solution(mesh):
    return jax.shard_map(
        on_device,
        mesh=mesh,
        in_specs=(
            P(("pipe", "head"), None),
            P(None, "pipe", "head"),
            P(None, None, "head"),
            P(),
            P(),
            P(),
            P("head", None),
            P(("pipe", "head"), None),
            P(),
        ),
        out_specs=P(("pipe", "head"), None),
        check_vma=False,
    )
```

```python
import math

import jax
import jax.numpy as jnp
from jax import lax
from jax.experimental import pallas as pl
from jax.experimental.pallas import tpu as pltpu
from jax.sharding import PartitionSpec as P

MESH = pl.DeviceIdType.MESH
HD = 128
HEADS = 3
W = HEADS * HD
PATCH = 128
NX, NZ, NY, NL, NC = 4, 2, 8, 4, 2
NH = NL * NC
HALF = PATCH // 2
TOK = PATCH // NH
OWN, TEXT, NEW = 0, NY, NY + 1
STAT = 32
D = 3072
CHUNKS = 3
CW = D // CHUNKS
BF, F32 = jnp.bfloat16, jnp.float32


def dot_nt(a, b):
    return lax.dot_general(a, b, (((1,), (1,)), ((), ())), preferred_element_type=F32)


def three_parts(rows):
    hi = rows.astype(BF).astype(F32)
    mid = (rows - hi).astype(BF).astype(F32)
    return jnp.concatenate([hi, mid, rows - hi - mid, jnp.zeros_like(rows)], axis=0).astype(BF)


def whole(parts):
    parts = parts.astype(F32)
    return parts[0:8] + parts[8:16] + parts[16:24]


def with_ones(values):
    return jnp.concatenate([values, jnp.ones_like(values)], axis=1)


def shares(stats):
    top = stats[0][0]
    for row, _ in stats[1:]:
        top = jnp.maximum(top, row)
    factors = [jnp.exp2(row - top) for row, _ in stats]
    total = factors[0] * stats[0][1]
    for factor, (_, part) in zip(factors[1:], stats[1:]):
        total = total + factor * part
    return top, factors, total


def diagonal(row, first):
    shape = (HALF, HD)
    on = lax.broadcasted_iota(jnp.int32, shape, 0) + first == lax.broadcasted_iota(jnp.int32, shape, 1)
    return jnp.where(on, row, 0.0).astype(BF)


def dot(a, b):
    return jnp.dot(a, b, preferred_element_type=F32)


def kernel(
    fresh, stale, text, tlen, qg_in, kg_in, w, hidden_in, gate_in, o_ref,
    qraw, kvraw, qall, kv, obuf, orecv, zsend, zrecv, attn, wv, psend, pown, precv, pfin, rsend, rrecv,
    qg, kg, hidden, gate,
    loc_sem, q_ssem, q_rsem, f_ssem, f_rsem, kv_ssem, kv_rsem, x_ssem, x_rsem, o_ssem, o_rsem, z_ssem, z_rsem,
    p_ssem, p_rsem, r_ssem, r_rsem,
):
    pipe, me = lax.axis_index("pipe"), lax.axis_index("head")
    x, zh, y = pipe // (NZ * NY), (pipe // NY) % NZ, pipe % NY
    zl, core = me // NC, me % NC

    def at_x(j):
        return ((((x + j) % NX) * NZ + zh) * NY + y, me)

    def at_y(j):
        return ((x * NZ + zh) * NY + (y + j) % NY, me)

    def at_head(r, i):
        return ((x * NZ + (zh + r) % NZ) * NY + y, (me + i) % NH)

    pair = (pipe, zl * NC + 1 - core)

    def remote(src, dst, ssem, rsem, dev):
        return pltpu.make_async_remote_copy(
            src_ref=src, dst_ref=dst, send_sem=ssem, recv_sem=rsem, device_id=dev, device_id_type=MESH
        )

    bar = pltpu.get_barrier_semaphore()
    partners = [at_x(j) for j in range(1, NX)] + [at_y(1), at_y(NY - 1)]
    partners += [at_head(r, i) for r in range(NZ) for i in range(NH) if (r, i) != (0, 0)]
    for dev in partners:
        pl.semaphore_signal(bar, inc=1, device_id=dev, device_id_type=MESH)

    share = x * NZ + zh
    get_w = pltpu.make_async_copy(w, wv, loc_sem.at[0])
    window = pl.ds(pl.multiple_of((share // 2) * 128, 128), 128)
    get_text = [
        pltpu.make_async_copy(text.at[:, window, pl.ds(h * HD, HD)], kv.at[h, TEXT], loc_sem.at[6 + HEADS + h])
        for h in range(HEADS)
    ]
    get_small = [
        pltpu.make_async_copy(src, dst, loc_sem.at[2 + n])
        for n, (src, dst) in enumerate(((qg_in, qg), (kg_in, kg), (hidden_in, hidden), (gate_in, gate)))
    ]
    get_own = [
        pltpu.make_async_copy(stale.at[:, :, pl.ds(h * HD, HD)], kv.at[h, OWN], loc_sem.at[6 + h])
        for h in range(HEADS)
    ]

    def head_cols(part, i):
        return fresh.at[:, pl.ds(pl.multiple_of(part * D + ((me + i) % NH) * W, W), W)]

    my_half, my_spot = ((zl + 1) // 2) % 2, (zl // 2) * NC + core

    def q_hop(r, i):
        return remote(
            head_cols(0, i), qraw.at[my_half, r, my_spot], q_ssem.at[r, i], q_rsem.at[r, i], at_head(r, i)
        )

    def f_hop(part, i):
        return remote(head_cols(part + 1, i), kvraw.at[part, i], f_ssem.at[part, i], f_rsem.at[part, i], at_head(0, i))

    q_local = pltpu.make_async_copy(head_cols(0, 0), qraw.at[my_half, 0, my_spot], q_rsem.at[0, 0])
    f_local = [
        pltpu.make_async_copy(head_cols(part + 1, 0), kvraw.at[part, 0], f_rsem.at[part, 0]) for part in range(2)
    ]
    q_local.start()
    for copy in get_small[:2]:
        copy.start()
    pl.semaphore_wait(bar, len(partners))

    for r in (1, 0):
        for i in range(NH):
            if (r, i) != (0, 0):
                q_hop(r, i).start()

    def hop(h, slot):
        if slot == 1 or slot == NY - 1:
            src = stale.at[:, :, pl.ds(h * HD, HD)]
        elif slot == 40:
            src = kv.at[h, 3, 0]
        elif slot == 41:
            src = kv.at[h, 5, 1]
        else:
            src = kv.at[h, slot - 1 if slot < 4 else slot + 1]
        if slot >= 40:
            dst = kv.at[h, 4, slot - 40]
        else:
            dst = kv.at[h, slot]
        sem = {40: 0, 41: 4}.get(slot, slot)
        up = slot < 4 or slot == 40
        return remote(src, dst, kv_ssem.at[h, sem], kv_rsem.at[h, sem], at_y(1 if up else NY - 1))

    for h in range(HEADS):
        hop(h, 1).start()
        hop(h, 7).start()

    for copy in [*get_own, *get_text, get_w, *get_small[2:]]:
        copy.start()

    for part in range(2):
        f_local[part].start()
        for i in range(1, NH):
            f_hop(part, i).start()

    for h in range(HEADS):
        hop(h, 1).wait_recv()
        hop(h, 2).start()
        hop(h, 7).wait_recv()
        hop(h, 6).start()

    scale = math.log2(math.e) / math.sqrt(HD)

    def normed(rows, gain):
        return (rows * lax.rsqrt(jnp.mean(rows * rows, axis=-1, keepdims=True) + 1e-06) * gain[...]).astype(BF)

    def x_hop(half, j):
        return remote(
            qall.at[half, 0], qall.at[half, NX - j], x_ssem.at[half, j], x_rsem.at[half, NX - j], at_x(j)
        )

    for copy in get_small[:2]:
        copy.wait()
    q_local.wait()
    for r in range(NZ):
        for i in range(NH):
            if (r, i) != (0, 0):
                q_hop(r, i).wait_recv()
    for half in range(2):
        for h in range(HEADS):
            rows = qraw[half, :, :, :, pl.ds(h * HD, HD)].reshape(PATCH, HD).astype(F32)
            qall[half, 0, h] = normed(rows, qg)
        for j in (2, 1, 3):
            x_hop(half, j).start()

    for h in range(HEADS):
        hop(h, 2).wait_recv()
        hop(h, 3).start()
        hop(h, 6).wait_recv()
        hop(h, 5).start()

    for part in range(2):
        f_local[part].wait()
        for i in range(1, NH):
            f_hop(part, i).wait_recv()
    for h in range(HEADS):
        cols = pl.ds(h * HD, HD)
        kv[h, NEW, 0] = normed(kvraw[0, :, :, cols].reshape(PATCH, HD).astype(F32), kg)
        kv[h, NEW, 1] = kvraw[1, :, :, cols].reshape(PATCH, HD)

    for h in range(HEADS):
        hop(h, 3).wait_recv()
        hop(h, 40).start()
        hop(h, 5).wait_recv()
        hop(h, 41).start()

    for copy in get_own + get_text:
        copy.wait()
    spot = lax.broadcasted_iota(jnp.int32, (1, 128), 1)
    live = (spot // 64 == share % 2) & (spot + (share // 2) * 128 < tlen[0])
    bias = jnp.where(live, 0.0, -1e30)

    def o_hop(half, h, j):
        return remote(
            obuf.at[half, h, j], orecv.at[half, h, NX - j], o_ssem.at[half, h, j], o_rsem.at[half, h, NX - j], at_x(j)
        )

    def z_hop(half):
        return remote(zsend.at[half], zrecv.at[half], z_ssem.at[half], z_rsem.at[half], at_head(1, 0))

    def attend(half, h):
        q = qall[half, :, h].reshape(NX * PATCH, HD)
        keys = kv[h, pl.ds(1, NY), 0].reshape(NY * PATCH, HD)
        values = kv[h, pl.ds(1, NY), 1].reshape(NY * PATCH, HD)
        scores = dot_nt(q, keys)
        split = (NY - 1) * PATCH
        scores = jnp.concatenate([scores[:, :split], scores[:, split:] + bias], axis=1)
        mine = jnp.concatenate([dot_nt(q[:HALF], kv[h, NEW, 0]), dot_nt(q[HALF:], kv[h, OWN, 0])], axis=0)
        top = jnp.maximum(jnp.max(scores, axis=-1, keepdims=True), jnp.max(mine, axis=-1, keepdims=True))
        e = jnp.exp2((scores - top) * scale).astype(BF)
        e_mine = jnp.exp2((mine - top) * scale).astype(BF)
        own = [dot(e_mine[:HALF], with_ones(kv[h, NEW, 1])), dot(e_mine[HALF:], with_ones(kv[h, OWN, 1]))]
        out = dot(e, with_ones(values)) + jnp.concatenate(own, axis=0)
        top = top * scale
        lane = lax.broadcasted_iota(jnp.int32, (PATCH, HD), 1)
        table = jnp.zeros((PATCH, HD), F32)
        for j in range(NX):
            rows = slice(j * PATCH, (j + 1) * PATCH)
            obuf[half, h, j, pl.ds(0, PATCH), :] = out[rows, :HD].astype(BF)
            table = jnp.where(lane == j, top[rows], jnp.where(lane == NX + j, out[rows, HD:], table))
        stats = three_parts(jnp.transpose(table)[0:8])
        for j in range(NX):
            obuf[half, h, j, pl.ds(PATCH, STAT), :] = stats
        for j in (2, 1, 3):
            o_hop(half, h, j).start()

    def sources(half, h):
        refs = [obuf.at[half, h, 0]] + [orecv.at[half, h, j] for j in range(1, NX)]
        stats = []
        for j, ref in enumerate(refs):
            rows, at = whole(ref[pl.ds(PATCH, STAT), :]), (NX - j) % NX
            stats.append((rows[at : at + 1], rows[NX + at : NX + at + 1]))
        return jnp.concatenate([ref[pl.ds(0, PATCH), :] for ref in refs], axis=0), stats

    def merge_x(half):
        for h in range(HEADS):
            for j in range(1, NX):
                o_hop(half, h, j).wait_recv()
            parts, stats = sources(half, h)
            top, factors, total = shares(stats)
            out = dot(jnp.concatenate([diagonal(f, HALF) for f in factors], axis=1), parts)
            zsend[half, h, pl.ds(0, HALF), :] = out.astype(BF)
            row = lax.broadcasted_iota(jnp.int32, (8, HD), 0)
            table = jnp.where(row == 0, top, jnp.where(row == 1, total, 0.0))
            zsend[half, h, pl.ds(HALF, STAT), :] = three_parts(pltpu.roll(table, HALF, 1))
        z_hop(half).start()

    def merge_z(half):
        z_hop(half).wait_recv()
        for h in range(HEADS):
            parts, stats = sources(half, h)
            far = whole(zrecv[half, h, pl.ds(HALF, STAT), :])
            _, factors, total = shares(stats + [(far[0:1], far[1:2])])
            inverse = 1.0 / total
            weights = [diagonal(f * inverse, 0) for f in factors]
            out = dot(jnp.concatenate(weights[:NX], axis=1), parts)
            out = out + dot(weights[NX][:, :HALF], zrecv[half, h, pl.ds(0, HALF), :])
            attn[half, :, :, pl.ds(h * HD, HD)] = out.astype(BF).reshape(NH // 2, TOK, HD)

    def p_hop(half, c):
        return remote(psend.at[half, c], precv.at[half, c], p_ssem.at[half, c], p_rsem.at[half, c], pair)

    def project(half):
        rows = jnp.concatenate([attn[half, n * NC + c] for c in (1 - core, core) for n in range(2)], axis=0)
        for c in range(CHUNKS):
            part = jnp.dot(rows, wv[:, pl.ds(c * CW, CW)], preferred_element_type=F32)
            psend[half, c] = part[: 2 * TOK].astype(BF)
            p_hop(half, c).start()
            pown[half, c] = part[2 * TOK :]

    def r_hop(half, c, n):
        owner = ((0, 3), (1, 2))[half][n]
        away = (owner + NL - zl) % NL
        return remote(
            rsend.at[half, c, n], rrecv.at[c, away], r_ssem.at[half, c, n], r_rsem.at[c, away], (pipe, owner * NC + core)
        )

    def arrived(c, away):
        return remote(rsend.at[0, c, 0], rrecv.at[c, away], r_ssem.at[0, c, 0], r_rsem.at[c, away], pair)

    def reduce(half):
        for c in range(CHUNKS):
            p_hop(half, c).wait_recv()
            both = pown[half, c] + precv[half, c].astype(F32)
            for n in range(2):
                owner = ((0, 3), (1, 2))[half][n]
                mine = both[n * TOK : (n + 1) * TOK]
                rsend[half, c, n] = mine.astype(BF)

                @pl.when(zl != owner)
                def _():
                    r_hop(half, c, n).start()

                @pl.when(zl == owner)
                def _():
                    pfin[c] = mine

    for half in range(2):
        for j in range(1, NX):
            x_hop(half, j).wait_recv()
        for h in range(HEADS):
            if half == 0:
                hop(h, 40).wait_recv()
                hop(h, 41).wait_recv()
            attend(half, h)
    merge_x(0)
    merge_x(1)
    merge_z(0)
    get_w.wait()
    project(0)
    reduce(0)
    merge_z(1)
    project(1)
    reduce(1)

    for copy in get_small[2:]:
        copy.wait()
    for c in range(CHUNKS):
        cols = pl.ds(c * CW, CW)
        for i in range(1, NL):
            arrived(c, i).wait_recv()
        total = pfin[c]
        for i in range(1, NL):
            total = total + rrecv[c, i].astype(F32)
        o_ref[:, cols] = (hidden[:, cols].astype(F32) + gate[:, cols] * total).astype(BF)

    for r in range(2):
        for i in range(NH):
            if (r, i) != (0, 0):
                q_hop(r, i).wait_send()
            if i > 0:
                f_hop(r, i).wait_send()
    for h in range(HEADS):
        for slot in (1, 2, 3, 40, 41, 5, 6, 7):
            hop(h, slot).wait_send()
    for half in range(2):
        for j in range(1, NX):
            x_hop(half, j).wait_send()
            for h in range(HEADS):
                o_hop(half, h, j).wait_send()
        z_hop(half).wait_send()
        for c in range(CHUNKS):
            p_hop(half, c).wait_send()
            for n in range(2):

                @pl.when(zl != ((0, 3), (1, 2))[half][n])
                def _():
                    r_hop(half, c, n).wait_send()


def on_device(fresh, stale, text, tlen, qg, kg, w, hidden, gate):
    dma = pltpu.SemaphoreType.DMA
    hbm, vmem = pl.BlockSpec(memory_space=pl.ANY), pl.BlockSpec(memory_space=pltpu.VMEM)
    return pl.pallas_call(
        kernel,
        out_shape=jax.ShapeDtypeStruct((TOK, D), BF),
        in_specs=[hbm, hbm, hbm, pl.BlockSpec(memory_space=pltpu.SMEM), hbm, hbm, hbm, hbm, hbm],
        out_specs=vmem,
        scratch_shapes=[
            pltpu.VMEM((2, NZ, NH // 2, TOK, W), BF),
            pltpu.VMEM((2, NH, TOK, W), BF),
            pltpu.VMEM((2, NX, HEADS, PATCH, HD), BF),
            pltpu.VMEM((HEADS, NY + 2, 2, PATCH, HD), BF),
            pltpu.VMEM((2, HEADS, NX, PATCH + STAT, HD), BF),
            pltpu.VMEM((2, HEADS, NX, PATCH + STAT, HD), BF),
            pltpu.VMEM((2, HEADS, HALF + STAT, HD), BF),
            pltpu.VMEM((2, HEADS, HALF + STAT, HD), BF),
            pltpu.VMEM((2, NH // 2, TOK, W), BF),
            pltpu.VMEM((W, D), BF),
            pltpu.VMEM((2, CHUNKS, 2 * TOK, CW), BF),
            pltpu.VMEM((2, CHUNKS, 2 * TOK, CW), F32),
            pltpu.VMEM((2, CHUNKS, 2 * TOK, CW), BF),
            pltpu.VMEM((CHUNKS, TOK, CW), F32),
            pltpu.VMEM((2, CHUNKS, 2, TOK, CW), BF),
            pltpu.VMEM((CHUNKS, NL, TOK, CW), BF),
            pltpu.VMEM((1, HD), F32),
            pltpu.VMEM((1, HD), F32),
            pltpu.VMEM((TOK, D), BF),
            pltpu.VMEM((1, D), F32),
            dma((6 + 2 * HEADS,)), dma((NZ, NH)), dma((NZ, NH)), dma((2, NH)), dma((2, NH)), dma((HEADS, NY)),
            dma((HEADS, NY)), dma((2, NX)), dma((2, NX)), dma((2, HEADS, NX)), dma((2, HEADS, NX)), dma((2,)), dma((2,)),
            dma((2, CHUNKS)), dma((2, CHUNKS)), dma((2, CHUNKS, 2)), dma((CHUNKS, NL)),
        ],
        name="joint_attention",
        cost_estimate=pl.CostEstimate(flops=2 * 10**9, bytes_accessed=4 * 10**6, transcendentals=4 * 10**6),
        compiler_params=pltpu.CompilerParams(
            collective_id=0, has_side_effects=True, vmem_limit_bytes=60 * 2**20
        ),
    )(fresh, stale, text, tlen, qg.reshape(1, HD), kg.reshape(1, HD), w, hidden, gate.reshape(1, D))


def solution(mesh):
    return jax.shard_map(
        on_device,
        mesh=mesh,
        in_specs=(
            P(("pipe", "head"), None),
            P(None, "pipe", "head"),
            P(None, None, "head"),
            P(),
            P(),
            P(),
            P("head", None),
            P(("pipe", "head"), None),
            P(),
        ),
        out_specs=P(("pipe", "head"), None),
        check_vma=False,
    )
```

```python
import math

import jax
import jax.numpy as jnp
from jax import lax
from jax.experimental import pallas as pl
from jax.experimental.pallas import tpu as pltpu
from jax.sharding import PartitionSpec as P

MESH = pl.DeviceIdType.MESH
HD = 128
HEADS = 3
W = HEADS * HD
PATCH = 128
NX, NZ, NY, NL, NC = 4, 2, 8, 4, 2
NH = NL * NC
HALF = PATCH // 2
TOK = PATCH // NH
OWN, TEXT, FAR, NEW = 0, 7, 8, 9
STAT = 32
D = 3072
CHUNKS = 3
CW = D // CHUNKS
BF, F32 = jnp.bfloat16, jnp.float32


def dot_nt(a, b):
    return lax.dot_general(a, b, (((1,), (1,)), ((), ())), preferred_element_type=F32)


def three_parts(rows):
    hi = rows.astype(BF).astype(F32)
    mid = (rows - hi).astype(BF).astype(F32)
    return jnp.concatenate([hi, mid, rows - hi - mid, jnp.zeros_like(rows)], axis=0).astype(BF)


def whole(parts):
    parts = parts.astype(F32)
    return parts[0:8] + parts[8:16] + parts[16:24]


def with_ones(values):
    return jnp.concatenate([values, jnp.ones_like(values)], axis=1)


def shares(stats):
    top = stats[0][0]
    for row, _ in stats[1:]:
        top = jnp.maximum(top, row)
    factors = [jnp.exp2(row - top) for row, _ in stats]
    total = factors[0] * stats[0][1]
    for factor, (_, part) in zip(factors[1:], stats[1:]):
        total = total + factor * part
    return top, factors, total


def diagonal(row, first):
    shape = (HALF, HD)
    on = lax.broadcasted_iota(jnp.int32, shape, 0) + first == lax.broadcasted_iota(jnp.int32, shape, 1)
    return jnp.where(on, row, 0.0).astype(BF)


def dot(a, b):
    return jnp.dot(a, b, preferred_element_type=F32)


def kernel(
    fresh, stale, text, tlen, qg_in, kg_in, w, hidden_in, gate_in, o_ref,
    qraw, kvraw, qall, kv, obuf, orecv, zsend, zrecv, attn, wv, psend, pown, precv, pfin, rsend, rrecv,
    qg, kg, hidden, gate,
    loc_sem, q_ssem, q_rsem, f_ssem, f_rsem, kv_ssem, kv_rsem, x_ssem, x_rsem, o_ssem, o_rsem, z_ssem, z_rsem,
    p_ssem, p_rsem, r_ssem, r_rsem,
):
    pipe, me = lax.axis_index("pipe"), lax.axis_index("head")
    x, zh, y = pipe // (NZ * NY), (pipe // NY) % NZ, pipe % NY
    zl, core = me // NC, me % NC

    def at_x(j):
        return ((((x + j) % NX) * NZ + zh) * NY + y, me)

    def at_y(j):
        return ((x * NZ + zh) * NY + (y + j) % NY, me)

    def at_head(r, i):
        return ((x * NZ + (zh + r) % NZ) * NY + y, (me + i) % NH)

    pair = (pipe, zl * NC + 1 - core)

    def remote(src, dst, ssem, rsem, dev):
        return pltpu.make_async_remote_copy(
            src_ref=src, dst_ref=dst, send_sem=ssem, recv_sem=rsem, device_id=dev, device_id_type=MESH
        )

    bar = pltpu.get_barrier_semaphore()
    partners = [at_x(j) for j in range(1, NX)] + [at_y(1), at_y(NY - 1)]
    partners += [at_head(r, i) for r in range(NZ) for i in range(NH) if (r, i) != (0, 0)]
    for dev in partners:
        pl.semaphore_signal(bar, inc=1, device_id=dev, device_id_type=MESH)

    share = x * NZ + zh
    get_w = pltpu.make_async_copy(w, wv, loc_sem.at[0])
    window = pl.ds(pl.multiple_of((share // 2) * 128, 128), 128)
    get_text = [
        pltpu.make_async_copy(text.at[:, window, pl.ds(h * HD, HD)], kv.at[h, TEXT], loc_sem.at[6 + HEADS + h])
        for h in range(HEADS)
    ]
    get_small = [
        pltpu.make_async_copy(src, dst, loc_sem.at[2 + n])
        for n, (src, dst) in enumerate(((qg_in, qg), (kg_in, kg), (hidden_in, hidden), (gate_in, gate)))
    ]
    get_own = [
        pltpu.make_async_copy(stale.at[:, :, pl.ds(h * HD, HD)], kv.at[h, OWN], loc_sem.at[6 + h])
        for h in range(HEADS)
    ]

    def head_cols(part, i):
        return fresh.at[:, pl.ds(pl.multiple_of(part * D + ((me + i) % NH) * W, W), W)]

    my_half, my_spot = ((zl + 1) // 2) % 2, (zl // 2) * NC + core

    def q_hop(r, i):
        return remote(
            head_cols(0, i), qraw.at[my_half, r, my_spot], q_ssem.at[r, i], q_rsem.at[r, i], at_head(r, i)
        )

    def f_hop(part, i):
        return remote(head_cols(part + 1, i), kvraw.at[part, i], f_ssem.at[part, i], f_rsem.at[part, i], at_head(0, i))

    q_local = pltpu.make_async_copy(head_cols(0, 0), qraw.at[my_half, 0, my_spot], q_rsem.at[0, 0])
    f_local = [
        pltpu.make_async_copy(head_cols(part + 1, 0), kvraw.at[part, 0], f_rsem.at[part, 0]) for part in range(2)
    ]
    q_local.start()
    for copy in get_small[:2]:
        copy.start()
    pl.semaphore_wait(bar, len(partners))

    for r in (1, 0):
        for i in range(NH):
            if (r, i) != (0, 0):
                q_hop(r, i).start()

    def hop(h, slot):
        up = slot in (1, 2, 3, 40)
        if slot in (1, 6):
            src = stale.at[:, :, pl.ds(h * HD, HD)]
        elif slot >= 40:
            src = kv.at[h, 3 if up else 4, slot - 40]
        else:
            src = kv.at[h, slot - 1 if up else slot + 1]
        dst = kv.at[h, FAR, slot - 40] if slot >= 40 else kv.at[h, slot]
        sem = {40: 0, 41: 7}.get(slot, slot)
        return remote(src, dst, kv_ssem.at[h, sem], kv_rsem.at[h, sem], at_y(1 if up else NY - 1))

    for h in range(HEADS):
        hop(h, 1).start()
        hop(h, 6).start()

    for copy in [*get_own, *get_text, get_w, *get_small[2:]]:
        copy.start()

    for part in range(2):
        f_local[part].start()
        for i in range(1, NH):
            f_hop(part, i).start()

    def relay(h, step):
        for slot, on in (((1, 2), (6, 5)), ((2, 3), (5, 4)), ((3, 40), (4, 41)))[step - 1]:
            hop(h, slot).wait_recv()
            hop(h, on).start()

    for h in range(HEADS):
        relay(h, 1)
    relay(0, 2)

    scale = math.log2(math.e) / math.sqrt(HD)

    def normed(rows, gain):
        return (rows * lax.rsqrt(jnp.mean(rows * rows, axis=-1, keepdims=True) + 1e-06) * gain[...]).astype(BF)

    def x_hop(half, j):
        return remote(
            qall.at[half, 0], qall.at[half, NX - j], x_ssem.at[half, j], x_rsem.at[half, NX - j], at_x(j)
        )

    for copy in get_small[:2]:
        copy.wait()
    q_local.wait()
    for r in range(NZ):
        for i in range(NH):
            if (r, i) != (0, 0):
                q_hop(r, i).wait_recv()
    def queries(half):
        for h in range(HEADS):
            rows = qraw[half, :, :, :, pl.ds(h * HD, HD)].reshape(PATCH, HD).astype(F32)
            qall[half, 0, h] = normed(rows, qg)
        for j in (2, 1, 3):
            x_hop(half, j).start()

    queries(0)
    relay(1, 2)
    relay(2, 2)
    queries(1)

    for part in range(2):
        f_local[part].wait()
        for i in range(1, NH):
            f_hop(part, i).wait_recv()
    for h in range(HEADS):
        cols = pl.ds(h * HD, HD)
        kv[h, NEW, 0] = normed(kvraw[0, :, :, cols].reshape(PATCH, HD).astype(F32), kg)
        kv[h, NEW, 1] = kvraw[1, :, :, cols].reshape(PATCH, HD)

    for h in range(HEADS):
        relay(h, 3)

    for copy in get_own + get_text:
        copy.wait()
    spot = lax.broadcasted_iota(jnp.int32, (1, 128), 1)
    live = (spot // 64 == share % 2) & (spot + (share // 2) * 128 < tlen[0])
    bias = jnp.where(live, 0.0, -1e30)

    def o_hop(half, h, j):
        return remote(
            obuf.at[half, h, j], orecv.at[half, h, NX - j], o_ssem.at[half, h, j], o_rsem.at[half, h, NX - j], at_x(j)
        )

    def z_hop(half):
        return remote(zsend.at[half], zrecv.at[half], z_ssem.at[half], z_rsem.at[half], at_head(1, 0))

    def scan(half, h, slots):
        q = qall[half, :, h].reshape(NX * PATCH, HD)
        keys = kv[h, pl.ds(1, slots), 0].reshape(slots * PATCH, HD)
        values = kv[h, pl.ds(1, slots), 1].reshape(slots * PATCH, HD)
        scores = dot_nt(q, keys)
        lo, hi = (TEXT - 1) * PATCH, TEXT * PATCH
        ends = [scores[:, hi:]] if slots > TEXT else []
        scores = jnp.concatenate([scores[:, :lo], scores[:, lo:hi] + bias, *ends], axis=1)
        mine = jnp.concatenate([dot_nt(q[:HALF], kv[h, NEW, 0]), dot_nt(q[HALF:], kv[h, OWN, 0])], axis=0)
        top = jnp.maximum(jnp.max(scores, axis=-1, keepdims=True), jnp.max(mine, axis=-1, keepdims=True))
        e = jnp.exp2((scores - top) * scale).astype(BF)
        e_mine = jnp.exp2((mine - top) * scale).astype(BF)
        own = [dot(e_mine[:HALF], with_ones(kv[h, NEW, 1])), dot(e_mine[HALF:], with_ones(kv[h, OWN, 1]))]
        return dot(e, with_ones(values)) + jnp.concatenate(own, axis=0), top

    def scan_far(half, h, out, top):
        q = qall[half, :, h].reshape(NX * PATCH, HD)
        scores = dot_nt(q, kv[h, FAR, 0])
        new_top = jnp.maximum(top, jnp.max(scores, axis=-1, keepdims=True))
        e = jnp.exp2((scores - new_top) * scale).astype(BF)
        return out * jnp.exp2((top - new_top) * scale) + dot(e, with_ones(kv[h, FAR, 1])), new_top

    def keep(half, h, out, top):
        top = top * scale
        lane = lax.broadcasted_iota(jnp.int32, (PATCH, HD), 1)
        table = jnp.zeros((PATCH, HD), F32)
        for j in range(NX):
            rows = slice(j * PATCH, (j + 1) * PATCH)
            obuf[half, h, j, pl.ds(0, PATCH), :] = out[rows, :HD].astype(BF)
            table = jnp.where(lane == j, top[rows], jnp.where(lane == NX + j, out[rows, HD:], table))
        stats = three_parts(jnp.transpose(table)[0:8])
        for j in range(NX):
            obuf[half, h, j, pl.ds(PATCH, STAT), :] = stats

    def send_out(half):
        for h in range(HEADS):
            for j in (2, 1, 3):
                o_hop(half, h, j).start()

    def sources(half, h):
        refs = [obuf.at[half, h, 0]] + [orecv.at[half, h, j] for j in range(1, NX)]
        stats = []
        for j, ref in enumerate(refs):
            rows, at = whole(ref[pl.ds(PATCH, STAT), :]), (NX - j) % NX
            stats.append((rows[at : at + 1], rows[NX + at : NX + at + 1]))
        return jnp.concatenate([ref[pl.ds(0, PATCH), :] for ref in refs], axis=0), stats

    def merge_x(half):
        for h in range(HEADS):
            for j in range(1, NX):
                o_hop(half, h, j).wait_recv()
        for h in range(HEADS):
            parts, stats = sources(half, h)
            top, factors, total = shares(stats)
            out = dot(jnp.concatenate([diagonal(f, HALF) for f in factors], axis=1), parts)
            zsend[half, h, pl.ds(0, HALF), :] = out.astype(BF)
            row = lax.broadcasted_iota(jnp.int32, (8, HD), 0)
            table = jnp.where(row == 0, top, jnp.where(row == 1, total, 0.0))
            zsend[half, h, pl.ds(HALF, STAT), :] = three_parts(pltpu.roll(table, HALF, 1))
        z_hop(half).start()

    def merge_z(half):
        z_hop(half).wait_recv()
        for h in range(HEADS):
            parts, stats = sources(half, h)
            far = whole(zrecv[half, h, pl.ds(HALF, STAT), :])
            _, factors, total = shares(stats + [(far[0:1], far[1:2])])
            inverse = 1.0 / total
            weights = [diagonal(f * inverse, 0) for f in factors]
            out = dot(jnp.concatenate(weights[:NX], axis=1), parts)
            out = out + dot(weights[NX][:, :HALF], zrecv[half, h, pl.ds(0, HALF), :])
            attn[half, :, :, pl.ds(h * HD, HD)] = out.astype(BF).reshape(NH // 2, TOK, HD)

    def p_hop(half, c):
        return remote(psend.at[half, c], precv.at[half, c], p_ssem.at[half, c], p_rsem.at[half, c], pair)

    def project(half):
        rows = jnp.concatenate([attn[half, n * NC + c] for c in (1 - core, core) for n in range(2)], axis=0)
        for c in range(CHUNKS):
            part = jnp.dot(rows, wv[:, pl.ds(c * CW, CW)], preferred_element_type=F32)
            psend[half, c] = part[: 2 * TOK].astype(BF)
            p_hop(half, c).start()
            pown[half, c] = part[2 * TOK :]

    def r_hop(half, c, n):
        owner = ((0, 3), (1, 2))[half][n]
        away = (owner + NL - zl) % NL
        return remote(
            rsend.at[half, c, n], rrecv.at[c, away], r_ssem.at[half, c, n], r_rsem.at[c, away], (pipe, owner * NC + core)
        )

    def arrived(c, away):
        return remote(rsend.at[0, c, 0], rrecv.at[c, away], r_ssem.at[0, c, 0], r_rsem.at[c, away], pair)

    def reduce(half):
        for c in range(CHUNKS):
            p_hop(half, c).wait_recv()
            both = pown[half, c] + precv[half, c].astype(F32)
            for n in range(2):
                owner = ((0, 3), (1, 2))[half][n]
                mine = both[n * TOK : (n + 1) * TOK]
                rsend[half, c, n] = mine.astype(BF)

                @pl.when(zl != owner)
                def _():
                    r_hop(half, c, n).start()

                @pl.when(zl == owner)
                def _():
                    pfin[c] = mine

    for j in range(1, NX):
        x_hop(0, j).wait_recv()
    partial = [scan(0, h, NY - 1) for h in range(HEADS)]
    for h in range(HEADS):
        hop(h, 40).wait_recv()
        hop(h, 41).wait_recv()
    for h in range(HEADS):
        keep(0, h, *scan_far(0, h, *partial[h]))
    send_out(0)
    for j in range(1, NX):
        x_hop(1, j).wait_recv()
    for h in range(HEADS):
        keep(1, h, *scan(1, h, NY))
    send_out(1)
    merge_x(0)
    merge_x(1)
    merge_z(0)
    get_w.wait()
    project(0)
    reduce(0)
    merge_z(1)
    project(1)
    reduce(1)

    for copy in get_small[2:]:
        copy.wait()
    for c in range(CHUNKS):
        cols = pl.ds(c * CW, CW)
        for i in range(1, NL):
            arrived(c, i).wait_recv()
        total = pfin[c]
        for i in range(1, NL):
            total = total + rrecv[c, i].astype(F32)
        o_ref[:, cols] = (hidden[:, cols].astype(F32) + gate[:, cols] * total).astype(BF)

    for r in range(2):
        for i in range(NH):
            if (r, i) != (0, 0):
                q_hop(r, i).wait_send()
            if i > 0:
                f_hop(r, i).wait_send()
    for h in range(HEADS):
        for slot in (1, 2, 3, 4, 5, 6, 40, 41):
            hop(h, slot).wait_send()
    for half in range(2):
        for j in range(1, NX):
            x_hop(half, j).wait_send()
            for h in range(HEADS):
                o_hop(half, h, j).wait_send()
        z_hop(half).wait_send()
        for c in range(CHUNKS):
            p_hop(half, c).wait_send()
            for n in range(2):

                @pl.when(zl != ((0, 3), (1, 2))[half][n])
                def _():
                    r_hop(half, c, n).wait_send()


def on_device(fresh, stale, text, tlen, qg, kg, w, hidden, gate):
    dma = pltpu.SemaphoreType.DMA
    hbm, vmem = pl.BlockSpec(memory_space=pl.ANY), pl.BlockSpec(memory_space=pltpu.VMEM)
    return pl.pallas_call(
        kernel,
        out_shape=jax.ShapeDtypeStruct((TOK, D), BF),
        in_specs=[hbm, hbm, hbm, pl.BlockSpec(memory_space=pltpu.SMEM), hbm, hbm, hbm, hbm, hbm],
        out_specs=vmem,
        scratch_shapes=[
            pltpu.VMEM((2, NZ, NH // 2, TOK, W), BF),
            pltpu.VMEM((2, NH, TOK, W), BF),
            pltpu.VMEM((2, NX, HEADS, PATCH, HD), BF),
            pltpu.VMEM((HEADS, NY + 2, 2, PATCH, HD), BF),
            pltpu.VMEM((2, HEADS, NX, PATCH + STAT, HD), BF),
            pltpu.VMEM((2, HEADS, NX, PATCH + STAT, HD), BF),
            pltpu.VMEM((2, HEADS, HALF + STAT, HD), BF),
            pltpu.VMEM((2, HEADS, HALF + STAT, HD), BF),
            pltpu.VMEM((2, NH // 2, TOK, W), BF),
            pltpu.VMEM((W, D), BF),
            pltpu.VMEM((2, CHUNKS, 2 * TOK, CW), BF),
            pltpu.VMEM((2, CHUNKS, 2 * TOK, CW), F32),
            pltpu.VMEM((2, CHUNKS, 2 * TOK, CW), BF),
            pltpu.VMEM((CHUNKS, TOK, CW), F32),
            pltpu.VMEM((2, CHUNKS, 2, TOK, CW), BF),
            pltpu.VMEM((CHUNKS, NL, TOK, CW), BF),
            pltpu.VMEM((1, HD), F32),
            pltpu.VMEM((1, HD), F32),
            pltpu.VMEM((TOK, D), BF),
            pltpu.VMEM((1, D), F32),
            dma((6 + 2 * HEADS,)), dma((NZ, NH)), dma((NZ, NH)), dma((2, NH)), dma((2, NH)), dma((HEADS, NY)),
            dma((HEADS, NY)), dma((2, NX)), dma((2, NX)), dma((2, HEADS, NX)), dma((2, HEADS, NX)), dma((2,)), dma((2,)),
            dma((2, CHUNKS)), dma((2, CHUNKS)), dma((2, CHUNKS, 2)), dma((CHUNKS, NL)),
        ],
        name="joint_attention",
        cost_estimate=pl.CostEstimate(flops=2 * 10**9, bytes_accessed=4 * 10**6, transcendentals=4 * 10**6),
        compiler_params=pltpu.CompilerParams(
            collective_id=0, has_side_effects=True, vmem_limit_bytes=60 * 2**20
        ),
    )(fresh, stale, text, tlen, qg.reshape(1, HD), kg.reshape(1, HD), w, hidden, gate.reshape(1, D))


def solution(mesh):
    return jax.shard_map(
        on_device,
        mesh=mesh,
        in_specs=(
            P(("pipe", "head"), None),
            P(None, "pipe", "head"),
            P(None, None, "head"),
            P(),
            P(),
            P(),
            P("head", None),
            P(("pipe", "head"), None),
            P(),
        ),
        out_specs=P(("pipe", "head"), None),
        check_vma=False,
    )
```

```python
import math

import jax
import jax.numpy as jnp
from jax import lax
from jax.experimental import pallas as pl
from jax.experimental.pallas import tpu as pltpu
from jax.sharding import PartitionSpec as P

MESH = pl.DeviceIdType.MESH
HD = 128
HEADS = 3
W = HEADS * HD
PATCH = 128
NX, NZ, NY, NL, NC = 4, 2, 8, 4, 2
NH = NL * NC
HALF = PATCH // 2
TOK = PATCH // NH
OWN, TEXT, FAR, NEW = 0, 7, 8, 9
STAT = 16
D = 3072
CHUNKS = 3
CW = D // CHUNKS
BF, F32 = jnp.bfloat16, jnp.float32


def dot_nt(a, b):
    return lax.dot_general(a, b, (((1,), (1,)), ((), ())), preferred_element_type=F32)


def stat_rows(top, total):
    at = lax.broadcasted_iota(jnp.int32, (8, HD), 0)
    rows = jnp.where(at < 3, top, total)
    hi = rows.astype(BF).astype(F32)
    mid = (rows - hi).astype(BF).astype(F32)
    part = at % 3
    rows = jnp.where(part == 0, hi, jnp.where(part == 1, mid, rows - hi - mid))
    return jnp.concatenate([rows, jnp.zeros_like(rows)], axis=0).astype(BF)


def whole(rows):
    rows = rows.astype(F32)
    return rows[0:1] + rows[1:2] + rows[2:3], rows[3:4] + rows[4:5] + rows[5:6]


def with_ones(values):
    return jnp.concatenate([values, jnp.ones_like(values)], axis=1)


def shares(stats):
    top = stats[0][0]
    for row, _ in stats[1:]:
        top = jnp.maximum(top, row)
    factors = [jnp.exp2(row - top) for row, _ in stats]
    total = factors[0] * stats[0][1]
    for factor, (_, part) in zip(factors[1:], stats[1:]):
        total = total + factor * part
    return top, factors, total


def diagonal(row, first):
    shape = (HALF, HD)
    on = lax.broadcasted_iota(jnp.int32, shape, 0) + first == lax.broadcasted_iota(jnp.int32, shape, 1)
    return jnp.where(on, row, 0.0).astype(BF)


def dot(a, b):
    return jnp.dot(a, b, preferred_element_type=F32)


def kernel(
    fresh, stale, text, tlen, qg_in, kg_in, w, hidden_in, gate_in, o_ref,
    qraw, kvraw, qall, kv, obuf, orecv, zsend, zrecv, attn, wv, psend, pown, precv, pfin, rsend, rrecv,
    qg, kg, hidden, gate,
    loc_sem, q_ssem, q_rsem, f_ssem, f_rsem, kv_ssem, kv_rsem, x_ssem, x_rsem, o_ssem, o_rsem, z_ssem, z_rsem,
    p_ssem, p_rsem, r_ssem, r_rsem,
):
    pipe, me = lax.axis_index("pipe"), lax.axis_index("head")
    x, zh, y = pipe // (NZ * NY), (pipe // NY) % NZ, pipe % NY
    zl, core = me // NC, me % NC

    def at_x(j):
        return ((((x + j) % NX) * NZ + zh) * NY + y, me)

    def at_y(j):
        return ((x * NZ + zh) * NY + (y + j) % NY, me)

    def at_head(r, i):
        return ((x * NZ + (zh + r) % NZ) * NY + y, (me + i) % NH)

    pair = (pipe, zl * NC + 1 - core)

    def remote(src, dst, ssem, rsem, dev):
        return pltpu.make_async_remote_copy(
            src_ref=src, dst_ref=dst, send_sem=ssem, recv_sem=rsem, device_id=dev, device_id_type=MESH
        )

    bar = pltpu.get_barrier_semaphore()
    partners = [at_x(j) for j in range(1, NX)] + [at_y(1), at_y(NY - 1)]
    partners += [at_head(r, i) for r in range(NZ) for i in range(NH) if (r, i) != (0, 0)]
    for dev in partners:
        pl.semaphore_signal(bar, inc=1, device_id=dev, device_id_type=MESH)

    share = x * NZ + zh
    get_w = pltpu.make_async_copy(w, wv, loc_sem.at[0])
    window = pl.ds(pl.multiple_of((share // 2) * 128, 128), 128)
    get_text = [
        pltpu.make_async_copy(text.at[:, window, pl.ds(h * HD, HD)], kv.at[h, TEXT], loc_sem.at[6 + HEADS + h])
        for h in range(HEADS)
    ]
    get_small = [
        pltpu.make_async_copy(src, dst, loc_sem.at[2 + n])
        for n, (src, dst) in enumerate(((qg_in, qg), (kg_in, kg), (hidden_in, hidden), (gate_in, gate)))
    ]
    get_own = [
        pltpu.make_async_copy(stale.at[:, :, pl.ds(h * HD, HD)], kv.at[h, OWN], loc_sem.at[6 + h])
        for h in range(HEADS)
    ]

    def head_cols(part, i):
        return fresh.at[:, pl.ds(pl.multiple_of(part * D + ((me + i) % NH) * W, W), W)]

    my_half, my_spot = ((zl + 1) // 2) % 2, (zl // 2) * NC + core

    def q_hop(r, i):
        return remote(
            head_cols(0, i), qraw.at[my_half, r, my_spot], q_ssem.at[r, i], q_rsem.at[r, i], at_head(r, i)
        )

    def f_hop(part, i):
        return remote(head_cols(part + 1, i), kvraw.at[part, i], f_ssem.at[part, i], f_rsem.at[part, i], at_head(0, i))

    q_local = pltpu.make_async_copy(head_cols(0, 0), qraw.at[my_half, 0, my_spot], q_rsem.at[0, 0])
    f_local = [
        pltpu.make_async_copy(head_cols(part + 1, 0), kvraw.at[part, 0], f_rsem.at[part, 0]) for part in range(2)
    ]
    q_local.start()
    for copy in get_small[:2]:
        copy.start()
    pl.semaphore_wait(bar, len(partners))

    for r in (1, 0):
        for i in range(NH):
            if (r, i) != (0, 0):
                q_hop(r, i).start()

    def hop(h, slot):
        up = slot in (1, 2, 3, 40)
        if slot in (1, 6):
            src = stale.at[:, :, pl.ds(h * HD, HD)]
        elif slot >= 40:
            src = kv.at[h, 3 if up else 4, slot - 40]
        else:
            src = kv.at[h, slot - 1 if up else slot + 1]
        dst = kv.at[h, FAR, slot - 40] if slot >= 40 else kv.at[h, slot]
        sem = {40: 0, 41: 7}.get(slot, slot)
        return remote(src, dst, kv_ssem.at[h, sem], kv_rsem.at[h, sem], at_y(1 if up else NY - 1))

    for h in range(HEADS):
        hop(h, 1).start()
        hop(h, 6).start()

    for copy in [*get_own, *get_text, get_w, *get_small[2:]]:
        copy.start()

    for part in range(2):
        f_local[part].start()
        for i in range(1, NH):
            f_hop(part, i).start()

    def relay(h, step):
        for slot, on in (((1, 2), (6, 5)), ((2, 3), (5, 4)), ((3, 40), (4, 41)))[step - 1]:
            hop(h, slot).wait_recv()
            hop(h, on).start()

    for h in range(HEADS):
        relay(h, 1)
    relay(0, 2)

    scale = math.log2(math.e) / math.sqrt(HD)

    def normed(rows, gain):
        return (rows * lax.rsqrt(jnp.mean(rows * rows, axis=-1, keepdims=True) + 1e-06) * gain[...]).astype(BF)

    def x_hop(half, j):
        return remote(
            qall.at[half, 0], qall.at[half, NX - j], x_ssem.at[half, j], x_rsem.at[half, NX - j], at_x(j)
        )

    for copy in get_small[:2]:
        copy.wait()
    q_local.wait()
    for r in range(NZ):
        for i in range(NH):
            if (r, i) != (0, 0):
                q_hop(r, i).wait_recv()
    def queries(half):
        for h in range(HEADS):
            rows = qraw[half, :, :, :, pl.ds(h * HD, HD)].reshape(PATCH, HD).astype(F32)
            qall[half, 0, h] = normed(rows, qg)
        for j in (2, 1, 3):
            x_hop(half, j).start()

    queries(0)
    relay(1, 2)
    relay(2, 2)
    queries(1)

    for part in range(2):
        f_local[part].wait()
        for i in range(1, NH):
            f_hop(part, i).wait_recv()
    for h in range(HEADS):
        cols = pl.ds(h * HD, HD)
        kv[h, NEW, 0] = normed(kvraw[0, :, :, cols].reshape(PATCH, HD).astype(F32), kg)
        kv[h, NEW, 1] = kvraw[1, :, :, cols].reshape(PATCH, HD)

    for h in range(HEADS):
        relay(h, 3)

    for copy in get_own + get_text:
        copy.wait()
    spot = lax.broadcasted_iota(jnp.int32, (1, 128), 1)
    live = (spot // 64 == share % 2) & (spot + (share // 2) * 128 < tlen[0])
    bias = jnp.where(live, 0.0, -1e30)

    def o_hop(half, h, j):
        return remote(
            obuf.at[half, h, j], orecv.at[half, h, NX - j], o_ssem.at[half, h, j], o_rsem.at[half, h, NX - j], at_x(j)
        )

    def z_hop(half):
        return remote(zsend.at[half], zrecv.at[half], z_ssem.at[half], z_rsem.at[half], at_head(1, 0))

    def scan(half, h):
        q = qall[half, :, h].reshape(NX * PATCH, HD)
        keys = kv[h, pl.ds(1, NY), 0].reshape(NY * PATCH, HD)
        values = kv[h, pl.ds(1, NY), 1].reshape(NY * PATCH, HD)
        scores = dot_nt(q, keys)
        lo, hi = (TEXT - 1) * PATCH, TEXT * PATCH
        scores = jnp.concatenate([scores[:, :lo], scores[:, lo:hi] + bias, scores[:, hi:]], axis=1)
        mine = jnp.concatenate([dot_nt(q[:HALF], kv[h, NEW, 0]), dot_nt(q[HALF:], kv[h, OWN, 0])], axis=0)
        top = jnp.maximum(jnp.max(scores, axis=-1, keepdims=True), jnp.max(mine, axis=-1, keepdims=True))
        e = jnp.exp2((scores - top) * scale).astype(BF)
        e_mine = jnp.exp2((mine - top) * scale).astype(BF)
        own = [dot(e_mine[:HALF], with_ones(kv[h, NEW, 1])), dot(e_mine[HALF:], with_ones(kv[h, OWN, 1]))]
        return dot(e, with_ones(values)) + jnp.concatenate(own, axis=0), top

    def send_out(half, h, out, top):
        top = top * scale
        lane = lax.broadcasted_iota(jnp.int32, (PATCH, HD), 1)
        table = jnp.zeros((PATCH, HD), F32)
        for j in range(NX):
            rows = slice(j * PATCH, (j + 1) * PATCH)
            obuf[half, h, j, pl.ds(0, PATCH), :] = out[rows, :HD].astype(BF)
            table = jnp.where(lane == j, top[rows], jnp.where(lane == NX + j, out[rows, HD:], table))
        rows = jnp.transpose(table)[0:8]
        for j in range(NX):
            stats = stat_rows(rows[j : j + 1], rows[NX + j : NX + j + 1])
            obuf[half, h, j, pl.ds(PATCH, STAT), :] = stats
        for j in (2, 1, 3):
            o_hop(half, h, j).start()

    def sources(half, h):
        refs = [obuf.at[half, h, 0]] + [orecv.at[half, h, j] for j in range(1, NX)]
        stats = [whole(ref[pl.ds(PATCH, STAT), :]) for ref in refs]
        return jnp.concatenate([ref[pl.ds(0, PATCH), :] for ref in refs], axis=0), stats

    def merge_x(half):
        for h in range(HEADS):
            for j in range(1, NX):
                o_hop(half, h, j).wait_recv()
        for h in range(HEADS):
            parts, stats = sources(half, h)
            top, factors, total = shares(stats)
            out = dot(jnp.concatenate([diagonal(f, HALF) for f in factors], axis=1), parts)
            zsend[half, h, pl.ds(0, HALF), :] = out.astype(BF)
            top, total = (pltpu.roll(jnp.broadcast_to(row, (8, HD)), HALF, 1) for row in (top, total))
            zsend[half, h, pl.ds(HALF, STAT), :] = stat_rows(top, total)
        z_hop(half).start()

    def merge_z(half):
        z_hop(half).wait_recv()
        for h in range(HEADS):
            parts, stats = sources(half, h)
            _, factors, total = shares(stats + [whole(zrecv[half, h, pl.ds(HALF, STAT), :])])
            inverse = 1.0 / total
            weights = [diagonal(f * inverse, 0) for f in factors]
            out = dot(jnp.concatenate(weights[:NX], axis=1), parts)
            out = out + dot(weights[NX][:, :HALF], zrecv[half, h, pl.ds(0, HALF), :])
            attn[half, :, :, pl.ds(h * HD, HD)] = out.astype(BF).reshape(NH // 2, TOK, HD)

    def p_hop(half, c):
        return remote(psend.at[half, c], precv.at[half, c], p_ssem.at[half, c], p_rsem.at[half, c], pair)

    def project(half):
        rows = jnp.concatenate([attn[half, n * NC + c] for c in (1 - core, core) for n in range(2)], axis=0)
        for c in range(CHUNKS):
            part = jnp.dot(rows, wv[:, pl.ds(c * CW, CW)], preferred_element_type=F32)
            psend[half, c] = part[: 2 * TOK].astype(BF)
            p_hop(half, c).start()
            pown[half, c] = part[2 * TOK :]

    def r_hop(half, c, n):
        owner = ((0, 3), (1, 2))[half][n]
        away = (owner + NL - zl) % NL
        return remote(
            rsend.at[half, c, n], rrecv.at[c, away], r_ssem.at[half, c, n], r_rsem.at[c, away], (pipe, owner * NC + core)
        )

    def arrived(c, away):
        return remote(rsend.at[0, c, 0], rrecv.at[c, away], r_ssem.at[0, c, 0], r_rsem.at[c, away], pair)

    def reduce(half):
        for c in range(CHUNKS):
            p_hop(half, c).wait_recv()
            both = pown[half, c] + precv[half, c].astype(F32)
            for n in range(2):
                owner = ((0, 3), (1, 2))[half][n]
                mine = both[n * TOK : (n + 1) * TOK]
                rsend[half, c, n] = mine.astype(BF)

                @pl.when(zl != owner)
                def _():
                    r_hop(half, c, n).start()

                @pl.when(zl == owner)
                def _():
                    pfin[c] = mine

    for j in range(1, NX):
        x_hop(0, j).wait_recv()
    for h in range(HEADS):
        hop(h, 40).wait_recv()
        hop(h, 41).wait_recv()
        send_out(0, h, *scan(0, h))
    for j in range(1, NX):
        x_hop(1, j).wait_recv()
    for h in range(HEADS):
        send_out(1, h, *scan(1, h))
    merge_x(0)
    merge_x(1)
    merge_z(0)
    get_w.wait()
    project(0)
    reduce(0)
    merge_z(1)
    project(1)
    reduce(1)

    for copy in get_small[2:]:
        copy.wait()
    for c in range(CHUNKS):
        cols = pl.ds(c * CW, CW)
        for i in range(1, NL):
            arrived(c, i).wait_recv()
        total = pfin[c]
        for i in range(1, NL):
            total = total + rrecv[c, i].astype(F32)
        o_ref[:, cols] = (hidden[:, cols].astype(F32) + gate[:, cols] * total).astype(BF)

    for r in range(2):
        for i in range(NH):
            if (r, i) != (0, 0):
                q_hop(r, i).wait_send()
            if i > 0:
                f_hop(r, i).wait_send()
    for h in range(HEADS):
        for slot in (1, 2, 3, 4, 5, 6, 40, 41):
            hop(h, slot).wait_send()
    for half in range(2):
        for j in range(1, NX):
            x_hop(half, j).wait_send()
            for h in range(HEADS):
                o_hop(half, h, j).wait_send()
        z_hop(half).wait_send()
        for c in range(CHUNKS):
            p_hop(half, c).wait_send()
            for n in range(2):

                @pl.when(zl != ((0, 3), (1, 2))[half][n])
                def _():
                    r_hop(half, c, n).wait_send()


def on_device(fresh, stale, text, tlen, qg, kg, w, hidden, gate):
    dma = pltpu.SemaphoreType.DMA
    hbm, vmem = pl.BlockSpec(memory_space=pl.ANY), pl.BlockSpec(memory_space=pltpu.VMEM)
    return pl.pallas_call(
        kernel,
        out_shape=jax.ShapeDtypeStruct((TOK, D), BF),
        in_specs=[hbm, hbm, hbm, pl.BlockSpec(memory_space=pltpu.SMEM), hbm, hbm, hbm, hbm, hbm],
        out_specs=vmem,
        scratch_shapes=[
            pltpu.VMEM((2, NZ, NH // 2, TOK, W), BF),
            pltpu.VMEM((2, NH, TOK, W), BF),
            pltpu.VMEM((2, NX, HEADS, PATCH, HD), BF),
            pltpu.VMEM((HEADS, NY + 2, 2, PATCH, HD), BF),
            pltpu.VMEM((2, HEADS, NX, PATCH + STAT, HD), BF),
            pltpu.VMEM((2, HEADS, NX, PATCH + STAT, HD), BF),
            pltpu.VMEM((2, HEADS, HALF + STAT, HD), BF),
            pltpu.VMEM((2, HEADS, HALF + STAT, HD), BF),
            pltpu.VMEM((2, NH // 2, TOK, W), BF),
            pltpu.VMEM((W, D), BF),
            pltpu.VMEM((2, CHUNKS, 2 * TOK, CW), BF),
            pltpu.VMEM((2, CHUNKS, 2 * TOK, CW), F32),
            pltpu.VMEM((2, CHUNKS, 2 * TOK, CW), BF),
            pltpu.VMEM((CHUNKS, TOK, CW), F32),
            pltpu.VMEM((2, CHUNKS, 2, TOK, CW), BF),
            pltpu.VMEM((CHUNKS, NL, TOK, CW), BF),
            pltpu.VMEM((1, HD), F32),
            pltpu.VMEM((1, HD), F32),
            pltpu.VMEM((TOK, D), BF),
            pltpu.VMEM((1, D), F32),
            dma((6 + 2 * HEADS,)), dma((NZ, NH)), dma((NZ, NH)), dma((2, NH)), dma((2, NH)), dma((HEADS, NY)),
            dma((HEADS, NY)), dma((2, NX)), dma((2, NX)), dma((2, HEADS, NX)), dma((2, HEADS, NX)), dma((2,)), dma((2,)),
            dma((2, CHUNKS)), dma((2, CHUNKS)), dma((2, CHUNKS, 2)), dma((CHUNKS, NL)),
        ],
        name="joint_attention",
        cost_estimate=pl.CostEstimate(flops=2 * 10**9, bytes_accessed=4 * 10**6, transcendentals=4 * 10**6),
        compiler_params=pltpu.CompilerParams(
            collective_id=0, has_side_effects=True, vmem_limit_bytes=60 * 2**20
        ),
    )(fresh, stale, text, tlen, qg.reshape(1, HD), kg.reshape(1, HD), w, hidden, gate.reshape(1, D))


def solution(mesh):
    return jax.shard_map(
        on_device,
        mesh=mesh,
        in_specs=(
            P(("pipe", "head"), None),
            P(None, "pipe", "head"),
            P(None, None, "head"),
            P(),
            P(),
            P(),
            P("head", None),
            P(("pipe", "head"), None),
            P(),
        ),
        out_specs=P(("pipe", "head"), None),
        check_vma=False,
    )
```

```python
import math

import jax
import jax.numpy as jnp
from jax import lax
from jax.experimental import pallas as pl
from jax.experimental.pallas import tpu as pltpu
from jax.sharding import PartitionSpec as P

MESH = pl.DeviceIdType.MESH
HD = 128
HEADS = 3
W = HEADS * HD
PATCH = 128
NX, NZ, NY, NL, NC = 4, 2, 8, 4, 2
NH = NL * NC
HALF = PATCH // 2
TOK = PATCH // NH
OWN, TEXT, FAR, NEW = 0, 7, 8, 9
STAT = 16
D = 3072
CHUNKS = 3
CW = D // CHUNKS
BF, F32 = jnp.bfloat16, jnp.float32


def dot_nt(a, b):
    return lax.dot_general(a, b, (((1,), (1,)), ((), ())), preferred_element_type=F32)


def stat_rows(top, total):
    at = lax.broadcasted_iota(jnp.int32, (8, HD), 0)
    rows = jnp.where(at < 3, top, total)
    hi = rows.astype(BF).astype(F32)
    mid = (rows - hi).astype(BF).astype(F32)
    part = at % 3
    rows = jnp.where(part == 0, hi, jnp.where(part == 1, mid, rows - hi - mid))
    return jnp.concatenate([rows, jnp.zeros_like(rows)], axis=0).astype(BF)


def whole(rows):
    rows = rows.astype(F32)
    return rows[0:1] + rows[1:2] + rows[2:3], rows[3:4] + rows[4:5] + rows[5:6]


def with_ones(values):
    return jnp.concatenate([values, jnp.ones_like(values)], axis=1)


def shares(stats):
    top = stats[0][0]
    for row, _ in stats[1:]:
        top = jnp.maximum(top, row)
    factors = [jnp.exp2(row - top) for row, _ in stats]
    total = factors[0] * stats[0][1]
    for factor, (_, part) in zip(factors[1:], stats[1:]):
        total = total + factor * part
    return top, factors, total


def diagonal(row, first):
    shape = (HALF, HD)
    on = lax.broadcasted_iota(jnp.int32, shape, 0) + first == lax.broadcasted_iota(jnp.int32, shape, 1)
    return jnp.where(on, row, 0.0).astype(BF)


def dot(a, b):
    return jnp.dot(a, b, preferred_element_type=F32)


def kernel(
    fresh, stale, text, tlen, qg_in, kg_in, w, hidden_in, gate_in, o_ref,
    qraw, kvraw, qall, kv, obuf, orecv, zsend, zrecv, attn, wv, psend, pown, precv, pfin, rsend, rrecv,
    qg, kg, hidden, gate,
    loc_sem, q_ssem, q_rsem, f_ssem, f_rsem, kv_ssem, kv_rsem, x_ssem, x_rsem, o_ssem, o_rsem, z_ssem, z_rsem,
    p_ssem, p_rsem, r_ssem, r_rsem,
):
    pipe, me = lax.axis_index("pipe"), lax.axis_index("head")
    x, zh, y = pipe // (NZ * NY), (pipe // NY) % NZ, pipe % NY
    zl, core = me // NC, me % NC

    def at_x(j):
        return ((((x + j) % NX) * NZ + zh) * NY + y, me)

    def at_y(j):
        return ((x * NZ + zh) * NY + (y + j) % NY, me)

    def at_head(r, i):
        return ((x * NZ + (zh + r) % NZ) * NY + y, (me + i) % NH)

    pair = (pipe, zl * NC + 1 - core)

    def remote(src, dst, ssem, rsem, dev):
        return pltpu.make_async_remote_copy(
            src_ref=src, dst_ref=dst, send_sem=ssem, recv_sem=rsem, device_id=dev, device_id_type=MESH
        )

    bar = pltpu.get_barrier_semaphore()
    partners = [at_x(j) for j in range(1, NX)] + [at_y(1), at_y(NY - 1)]
    partners += [at_head(r, i) for r in range(NZ) for i in range(NH) if (r, i) != (0, 0)]
    for dev in partners:
        pl.semaphore_signal(bar, inc=1, device_id=dev, device_id_type=MESH)

    share = x * NZ + zh
    get_w = pltpu.make_async_copy(w, wv, loc_sem.at[0])
    window = pl.ds(pl.multiple_of((share // 2) * 128, 128), 128)
    get_text = [
        pltpu.make_async_copy(text.at[:, window, pl.ds(h * HD, HD)], kv.at[h, TEXT], loc_sem.at[6 + HEADS + h])
        for h in range(HEADS)
    ]
    get_small = [
        pltpu.make_async_copy(src, dst, loc_sem.at[2 + n])
        for n, (src, dst) in enumerate(((qg_in, qg), (kg_in, kg), (hidden_in, hidden), (gate_in, gate)))
    ]
    get_own = [
        pltpu.make_async_copy(stale.at[:, :, pl.ds(h * HD, HD)], kv.at[h, OWN], loc_sem.at[6 + h])
        for h in range(HEADS)
    ]

    def head_cols(part, i):
        return fresh.at[:, pl.ds(pl.multiple_of(part * D + ((me + i) % NH) * W, W), W)]

    my_half, my_spot = ((zl + 1) // 2) % 2, (zl // 2) * NC + core

    def q_hop(r, i):
        return remote(
            head_cols(0, i), qraw.at[my_half, r, my_spot], q_ssem.at[r, i], q_rsem.at[r, i], at_head(r, i)
        )

    def f_hop(part, i):
        return remote(head_cols(part + 1, i), kvraw.at[part, i], f_ssem.at[part, i], f_rsem.at[part, i], at_head(0, i))

    q_local = pltpu.make_async_copy(head_cols(0, 0), qraw.at[my_half, 0, my_spot], q_rsem.at[0, 0])
    f_local = [
        pltpu.make_async_copy(head_cols(part + 1, 0), kvraw.at[part, 0], f_rsem.at[part, 0]) for part in range(2)
    ]
    q_local.start()
    for copy in get_small[:2]:
        copy.start()
    pl.semaphore_wait(bar, len(partners))

    for r in (1, 0):
        for i in range(NH):
            if (r, i) != (0, 0):
                q_hop(r, i).start()

    def hop(h, slot):
        up = slot in (1, 2, 3, 40)
        if slot in (1, 6):
            src = stale.at[:, :, pl.ds(h * HD, HD)]
        elif slot >= 40:
            src = kv.at[h, 3 if up else 4, slot - 40]
        else:
            src = kv.at[h, slot - 1 if up else slot + 1]
        dst = kv.at[h, FAR, slot - 40] if slot >= 40 else kv.at[h, slot]
        sem = {40: 0, 41: 7}.get(slot, slot)
        return remote(src, dst, kv_ssem.at[h, sem], kv_rsem.at[h, sem], at_y(1 if up else NY - 1))

    for h in range(HEADS):
        hop(h, 1).start()
        hop(h, 6).start()

    for copy in [*get_own, *get_text, get_w, *get_small[2:]]:
        copy.start()

    for part in range(2):
        f_local[part].start()
        for i in range(1, NH):
            f_hop(part, i).start()

    def relay(h, step):
        for slot, on in (((1, 2), (6, 5)), ((2, 3), (5, 4)), ((3, 40), (4, 41)))[step - 1]:
            hop(h, slot).wait_recv()
            hop(h, on).start()

    for h in range(HEADS):
        relay(h, 1)
    relay(0, 2)

    scale = math.log2(math.e) / math.sqrt(HD)

    def normed(rows, gain):
        return (rows * lax.rsqrt(jnp.mean(rows * rows, axis=-1, keepdims=True) + 1e-06) * gain[...]).astype(BF)

    def x_hop(half, j):
        return remote(
            qall.at[half, 0], qall.at[half, NX - j], x_ssem.at[half, j], x_rsem.at[half, NX - j], at_x(j)
        )

    for copy in get_small[:2]:
        copy.wait()
    q_local.wait()
    for r in range(NZ):
        for i in range(NH):
            if (r, i) != (0, 0):
                q_hop(r, i).wait_recv()
    def queries(half):
        for h in range(HEADS):
            rows = qraw[half, :, :, :, pl.ds(h * HD, HD)].reshape(PATCH, HD).astype(F32)
            qall[half, 0, h] = normed(rows, qg)
        for j in (2, 1, 3):
            x_hop(half, j).start()

    queries(0)
    relay(1, 2)
    relay(2, 2)
    queries(1)

    for part in range(2):
        f_local[part].wait()
        for i in range(1, NH):
            f_hop(part, i).wait_recv()
    for h in range(HEADS):
        cols = pl.ds(h * HD, HD)
        kv[h, NEW, 0] = normed(kvraw[0, :, :, cols].reshape(PATCH, HD).astype(F32), kg)
        kv[h, NEW, 1] = kvraw[1, :, :, cols].reshape(PATCH, HD)

    for h in range(HEADS):
        relay(h, 3)

    for copy in get_own + get_text:
        copy.wait()
    spot = lax.broadcasted_iota(jnp.int32, (1, 128), 1)
    live = (spot // 64 == share % 2) & (spot + (share // 2) * 128 < tlen[0])
    bias = jnp.where(live, 0.0, -1e30)

    def o_hop(half, h, j):
        return remote(
            obuf.at[half, h, j], orecv.at[half, h, NX - j], o_ssem.at[half, h, j], o_rsem.at[half, h, NX - j], at_x(j)
        )

    def z_hop(half, h):
        return remote(
            zsend.at[half, h], zrecv.at[half, h], z_ssem.at[half, h], z_rsem.at[half, h], at_head(1, 0)
        )

    def scan(half, h):
        q = qall[half, :, h].reshape(NX * PATCH, HD)
        keys = kv[h, pl.ds(1, NY), 0].reshape(NY * PATCH, HD)
        values = kv[h, pl.ds(1, NY), 1].reshape(NY * PATCH, HD)
        scores = dot_nt(q, keys)
        lo, hi = (TEXT - 1) * PATCH, TEXT * PATCH
        scores = jnp.concatenate([scores[:, :lo], scores[:, lo:hi] + bias, scores[:, hi:]], axis=1)
        mine = jnp.concatenate([dot_nt(q[:HALF], kv[h, NEW, 0]), dot_nt(q[HALF:], kv[h, OWN, 0])], axis=0)
        top = jnp.maximum(jnp.max(scores, axis=-1, keepdims=True), jnp.max(mine, axis=-1, keepdims=True))
        e = jnp.exp2((scores - top) * scale).astype(BF)
        e_mine = jnp.exp2((mine - top) * scale).astype(BF)
        own = [dot(e_mine[:HALF], with_ones(kv[h, NEW, 1])), dot(e_mine[HALF:], with_ones(kv[h, OWN, 1]))]
        return dot(e, with_ones(values)) + jnp.concatenate(own, axis=0), top

    def send_out(half, h, out, top):
        top = top * scale
        lane = lax.broadcasted_iota(jnp.int32, (PATCH, HD), 1)
        table = jnp.zeros((PATCH, HD), F32)
        for j in range(NX):
            rows = slice(j * PATCH, (j + 1) * PATCH)
            obuf[half, h, j, pl.ds(0, PATCH), :] = out[rows, :HD].astype(BF)
            table = jnp.where(lane == j, top[rows], jnp.where(lane == NX + j, out[rows, HD:], table))
        rows = jnp.transpose(table)[0:8]
        for j in range(NX):
            stats = stat_rows(rows[j : j + 1], rows[NX + j : NX + j + 1])
            obuf[half, h, j, pl.ds(PATCH, STAT), :] = stats
        for j in (2, 1, 3):
            o_hop(half, h, j).start()

    def sources(half, h):
        refs = [obuf.at[half, h, 0]] + [orecv.at[half, h, j] for j in range(1, NX)]
        stats = [whole(ref[pl.ds(PATCH, STAT), :]) for ref in refs]
        return jnp.concatenate([ref[pl.ds(0, PATCH), :] for ref in refs], axis=0), stats

    def merge_x(half):
        for h in range(HEADS):
            for j in range(1, NX):
                o_hop(half, h, j).wait_recv()
            parts, stats = sources(half, h)
            top, factors, total = shares(stats)
            out = dot(jnp.concatenate([diagonal(f, HALF) for f in factors], axis=1), parts)
            zsend[half, h, pl.ds(0, HALF), :] = out.astype(BF)
            top, total = (pltpu.roll(jnp.broadcast_to(row, (8, HD)), HALF, 1) for row in (top, total))
            zsend[half, h, pl.ds(HALF, STAT), :] = stat_rows(top, total)
            z_hop(half, h).start()

    def merge_z(half):
        for h in range(HEADS):
            z_hop(half, h).wait_recv()
            parts, stats = sources(half, h)
            _, factors, total = shares(stats + [whole(zrecv[half, h, pl.ds(HALF, STAT), :])])
            inverse = 1.0 / total
            weights = [diagonal(f * inverse, 0) for f in factors]
            out = dot(jnp.concatenate(weights[:NX], axis=1), parts)
            out = out + dot(weights[NX][:, :HALF], zrecv[half, h, pl.ds(0, HALF), :])
            attn[half, :, :, pl.ds(h * HD, HD)] = out.astype(BF).reshape(NH // 2, TOK, HD)

    def p_hop(half, c):
        return remote(psend.at[half, c], precv.at[half, c], p_ssem.at[half, c], p_rsem.at[half, c], pair)

    def project(half):
        rows = jnp.concatenate([attn[half, n * NC + c] for c in (1 - core, core) for n in range(2)], axis=0)
        for c in range(CHUNKS):
            part = jnp.dot(rows, wv[:, pl.ds(c * CW, CW)], preferred_element_type=F32)
            psend[half, c] = part[: 2 * TOK].astype(BF)
            p_hop(half, c).start()
            pown[half, c] = part[2 * TOK :]

    def r_hop(half, c, n):
        owner = ((0, 3), (1, 2))[half][n]
        away = (owner + NL - zl) % NL
        return remote(
            rsend.at[half, c, n], rrecv.at[c, away], r_ssem.at[half, c, n], r_rsem.at[c, away], (pipe, owner * NC + core)
        )

    def arrived(c, away):
        return remote(rsend.at[0, c, 0], rrecv.at[c, away], r_ssem.at[0, c, 0], r_rsem.at[c, away], pair)

    def reduce(half):
        for c in range(CHUNKS):
            p_hop(half, c).wait_recv()
            both = pown[half, c] + precv[half, c].astype(F32)
            for n in range(2):
                owner = ((0, 3), (1, 2))[half][n]
                mine = both[n * TOK : (n + 1) * TOK]
                rsend[half, c, n] = mine.astype(BF)

                @pl.when(zl != owner)
                def _():
                    r_hop(half, c, n).start()

                @pl.when(zl == owner)
                def _():
                    pfin[c] = mine

    for j in range(1, NX):
        x_hop(0, j).wait_recv()
    for h in range(HEADS):
        hop(h, 40).wait_recv()
        hop(h, 41).wait_recv()
        send_out(0, h, *scan(0, h))
    for j in range(1, NX):
        x_hop(1, j).wait_recv()
    for h in range(HEADS):
        send_out(1, h, *scan(1, h))
    merge_x(0)
    merge_x(1)
    merge_z(0)
    get_w.wait()
    project(0)
    reduce(0)
    merge_z(1)
    project(1)
    reduce(1)

    for copy in get_small[2:]:
        copy.wait()
    for c in range(CHUNKS):
        cols = pl.ds(c * CW, CW)
        for i in range(1, NL):
            arrived(c, i).wait_recv()
        total = pfin[c]
        for i in range(1, NL):
            total = total + rrecv[c, i].astype(F32)
        o_ref[:, cols] = (hidden[:, cols].astype(F32) + gate[:, cols] * total).astype(BF)

    for r in range(2):
        for i in range(NH):
            if (r, i) != (0, 0):
                q_hop(r, i).wait_send()
            if i > 0:
                f_hop(r, i).wait_send()
    for h in range(HEADS):
        for slot in (1, 2, 3, 4, 5, 6, 40, 41):
            hop(h, slot).wait_send()
    for half in range(2):
        for j in range(1, NX):
            x_hop(half, j).wait_send()
            for h in range(HEADS):
                o_hop(half, h, j).wait_send()
        for h in range(HEADS):
            z_hop(half, h).wait_send()
        for c in range(CHUNKS):
            p_hop(half, c).wait_send()
            for n in range(2):

                @pl.when(zl != ((0, 3), (1, 2))[half][n])
                def _():
                    r_hop(half, c, n).wait_send()


def on_device(fresh, stale, text, tlen, qg, kg, w, hidden, gate):
    dma = pltpu.SemaphoreType.DMA
    hbm, vmem = pl.BlockSpec(memory_space=pl.ANY), pl.BlockSpec(memory_space=pltpu.VMEM)
    return pl.pallas_call(
        kernel,
        out_shape=jax.ShapeDtypeStruct((TOK, D), BF),
        in_specs=[hbm, hbm, hbm, pl.BlockSpec(memory_space=pltpu.SMEM), hbm, hbm, hbm, hbm, hbm],
        out_specs=vmem,
        scratch_shapes=[
            pltpu.VMEM((2, NZ, NH // 2, TOK, W), BF),
            pltpu.VMEM((2, NH, TOK, W), BF),
            pltpu.VMEM((2, NX, HEADS, PATCH, HD), BF),
            pltpu.VMEM((HEADS, NY + 2, 2, PATCH, HD), BF),
            pltpu.VMEM((2, HEADS, NX, PATCH + STAT, HD), BF),
            pltpu.VMEM((2, HEADS, NX, PATCH + STAT, HD), BF),
            pltpu.VMEM((2, HEADS, HALF + STAT, HD), BF),
            pltpu.VMEM((2, HEADS, HALF + STAT, HD), BF),
            pltpu.VMEM((2, NH // 2, TOK, W), BF),
            pltpu.VMEM((W, D), BF),
            pltpu.VMEM((2, CHUNKS, 2 * TOK, CW), BF),
            pltpu.VMEM((2, CHUNKS, 2 * TOK, CW), F32),
            pltpu.VMEM((2, CHUNKS, 2 * TOK, CW), BF),
            pltpu.VMEM((CHUNKS, TOK, CW), F32),
            pltpu.VMEM((2, CHUNKS, 2, TOK, CW), BF),
            pltpu.VMEM((CHUNKS, NL, TOK, CW), BF),
            pltpu.VMEM((1, HD), F32),
            pltpu.VMEM((1, HD), F32),
            pltpu.VMEM((TOK, D), BF),
            pltpu.VMEM((1, D), F32),
            dma((6 + 2 * HEADS,)), dma((NZ, NH)), dma((NZ, NH)), dma((2, NH)), dma((2, NH)), dma((HEADS, NY)),
            dma((HEADS, NY)), dma((2, NX)), dma((2, NX)), dma((2, HEADS, NX)), dma((2, HEADS, NX)), dma((2, HEADS)),
            dma((2, HEADS)),
            dma((2, CHUNKS)), dma((2, CHUNKS)), dma((2, CHUNKS, 2)), dma((CHUNKS, NL)),
        ],
        name="joint_attention",
        cost_estimate=pl.CostEstimate(flops=2 * 10**9, bytes_accessed=4 * 10**6, transcendentals=4 * 10**6),
        compiler_params=pltpu.CompilerParams(
            collective_id=0, has_side_effects=True, vmem_limit_bytes=60 * 2**20
        ),
    )(fresh, stale, text, tlen, qg.reshape(1, HD), kg.reshape(1, HD), w, hidden, gate.reshape(1, D))


def solution(mesh):
    return jax.shard_map(
        on_device,
        mesh=mesh,
        in_specs=(
            P(("pipe", "head"), None),
            P(None, "pipe", "head"),
            P(None, None, "head"),
            P(),
            P(),
            P(),
            P("head", None),
            P(("pipe", "head"), None),
            P(),
        ),
        out_specs=P(("pipe", "head"), None),
        check_vma=False,
    )
```
